256 devices in a mesh: gy: 64 (over y, z_lo, x, core), gz: 4 (over z_hi).
Axes of the slice: x: 4, y: 4, z: 8 (z_hi: 4, z_lo: 2; z = z_hi * 2 + z_lo), core: 2. Of those that a mesh axis runs over, the one named last changes fastest.
Arguments:
- density: float32 [256, 1024, 1024], P(None, 'gy', 'gz'), may hold values from -16 to 16
Outputs:
- side_view: float32 [3, 256, 1024], P(None, 'gy', 'gz')
- top_view: float32 [3, 256, 1024], P(None, 'gz', 'gy')
The draws below stay inside these ranges and needn't reach their ends.
All inputs are finite; a program needn't handle non-finite values.
Results may differ from the reference program's by a relative error of at most 0.0003.
Values sent between devices are 32-bit elements; how exact they have to be, the bound alone decides.
A program may use at most 64 MiB of HBM per device.

```python
import math
import jax
import jax.numpy as jnp
from jax import lax

NX = 256
NY = 1024
NZ = 1024


def raised(drawn, own_key, source, target, shards_of, factor):
    owner, partner = [(jnp.arange(drawn.shape[axis_at]) // (drawn.shape[axis_at] // shards_of)).reshape([-1 if axis == axis_at else 1 for axis in range(drawn.ndim)]) for axis_at in (source, target)]
    chosen = jax.random.permutation(own_key, shards_of)[partner]
    strong = (owner == chosen) | (owner == (partner + shards_of // 2) % shards_of)
    return jnp.where(strong, factor * drawn, drawn)


def shard_levels(rng, dims, split, least, top_value):
    loudness, own = 1.0, jax.random.fold_in(rng, 6)
    for position, shards_of in split:
        draws = jnp.exp(jax.random.uniform(jax.random.fold_in(own, position), (shards_of,), jnp.float32, least / len(split), top_value / len(split)))
        loudness = loudness * jnp.repeat(draws, dims[position] // shards_of).reshape([-1 if axis == position else 1 for axis in range(len(dims))])
    return loudness


def bell_draw_with(rng, shape, width, most, split, heavy, kind=jnp.bfloat16):
    result = width * jax.random.normal(rng, shape, jnp.float32)
    if split:
        result = result * shard_levels(rng, shape, split, -0.22, 0.18)
    return jnp.clip(raised(result, jax.random.fold_in(rng, 3), *heavy), -most, most).astype(kind)


def setup_inputs(seed: int = 0) -> dict:
    key_list = jax.random.split(jax.random.key(seed), 2)
    return {
        "density": bell_draw_with(key_list[0], (NX, NY, NZ), 1.0, 16.0, ((1, 64), (2, 4)), (1, 0, 64, 4.0), jnp.float32),
    }


def plane_maps(center_row, lower_row, upper_row):
    padded = jnp.pad(center_row, 1)
    y_high = padded[2:, 1:-1]
    y_low = padded[:-2, 1:-1]
    z_high = padded[1:-1, 2:]
    z_low = padded[1:-1, :-2]
    grad_x = (upper_row - lower_row) * 0.5
    grad_y = (y_high - y_low) * 0.5
    grad_z = (z_high - z_low) * 0.5
    curve_x = upper_row + lower_row - 2.0 * center_row
    curve_y = y_high + y_low - 2.0 * center_row
    curve_z = z_high + z_low - 2.0 * center_row
    side_map = jnp.stack([grad_z.sum(0), grad_x.sum(0), (curve_x + curve_z).sum(0)])
    top_map = jnp.stack([grad_y.sum(1), grad_x.sum(1), (curve_x + curve_y).sum(1)])
    return (side_map, top_map)

def reference(density):

    def one_row(row_index):
        center_row = lax.dynamic_index_in_dim(density, row_index, 0, keepdims=False)
        lower_index = jnp.maximum(row_index - 1, 0).astype(jnp.int32)
        upper_index = jnp.minimum(row_index + 1, NX - 1).astype(jnp.int32)
        lower_row = lax.dynamic_index_in_dim(density, lower_index, 0, keepdims=False) * (row_index > 0).astype(density.dtype)
        upper_row = lax.dynamic_index_in_dim(density, upper_index, 0, keepdims=False) * (row_index < NX - 1).astype(density.dtype)
        return plane_maps(center_row, lower_row, upper_row)
    side_rows, top_rows = lax.map(one_row, jnp.arange(NX, dtype=jnp.int32))
    side_view = jnp.transpose(side_rows, (1, 0, 2)) * (1.0 / math.sqrt(NY))
    top_view = jnp.transpose(top_rows, (1, 0, 2)) * (1.0 / math.sqrt(NZ))
    return (side_view, top_view)
```

```python
import functools
import math

import jax
import jax.numpy as jnp
from jax import lax
from jax.experimental import pallas as pl
from jax.experimental.pallas import tpu as pltpu
from jax.sharding import PartitionSpec as P

MESH = pl.DeviceIdType.MESH
CHUNKS = 4
ORDER = (2, 1, 3, 0)


def iota(axis):
    return lax.broadcasted_iota(jnp.int32, (8, 128), axis)


def side_maps(total, low_x, high_x, low_z, high_z, factor):
    row, lane = iota(0), iota(1)
    lower_x = jnp.where(row % 4 == 0, pltpu.roll(low_x, 5, 0), pltpu.roll(total, 1, 0))
    upper_x = jnp.where(row % 4 == 3, pltpu.roll(high_x, 3, 0), pltpu.roll(total, 7, 0))
    down = pltpu.roll(total, 1, 1)
    up = pltpu.roll(total, 127, 1)
    low_edge = pltpu.roll(jnp.where(row >= 4, low_z, total), 4, 0)
    high_edge = pltpu.roll(jnp.where(row < 4, high_z, total), 4, 0)
    lower_z = jnp.where(lane == 0, pltpu.roll(low_edge, 1, 1), down)
    upper_z = jnp.where(lane == 127, pltpu.roll(high_edge, 127, 1), up)
    grad_z = (upper_z - lower_z) * (0.5 * factor)
    grad_x = (upper_x - lower_x) * (0.5 * factor)
    curve = (upper_x + lower_x + upper_z + lower_z - 4.0 * total) * factor
    return grad_z, grad_x, curve


def top_maps(total, low_y, high_y, low_x, high_x, factor):
    row, lane = iota(0), iota(1)
    lower_x = jnp.where(lane % 64 == 0, pltpu.roll(low_x, 65, 1), pltpu.roll(total, 1, 1))
    upper_x = jnp.where(lane % 64 == 63, pltpu.roll(high_x, 63, 1), pltpu.roll(total, 127, 1))
    low_edge = pltpu.roll(jnp.where(lane >= 64, low_y, total), 64, 1)
    high_edge = pltpu.roll(jnp.where(lane < 64, high_y, total), 64, 1)
    lower_y = pltpu.roll(jnp.where(row == 7, low_edge, total), 1, 0)
    upper_y = pltpu.roll(jnp.where(row == 0, high_edge, total), 7, 0)
    grad_y = (upper_y - lower_y) * (0.5 * factor)
    grad_x = (upper_x - lower_x) * (0.5 * factor)
    curve = (upper_x + lower_x + upper_y + lower_y - 4.0 * total) * factor
    return grad_y, grad_x, curve


def kernel(ny, nz, y_factor, z_factor, density, side_out, top_out, cells, side_part, side_recv, side_halo, top_part,
           top_recv, top_halo, load_sem, send_sem, recv_sem):
    rows, depth, width = cells.shape
    span = ny // CHUNKS
    chunk_rows = rows // CHUNKS
    me_y, me_z = lax.axis_index("gy"), lax.axis_index("gz")
    order = [lax.rem(me_y // span + step, CHUNKS) for step in ORDER]
    loads = []
    for step, chunk in enumerate(order):
        at = pl.ds(chunk * chunk_rows, chunk_rows)
        loads.append(pltpu.make_async_copy(density.at[at], cells.at[at], load_sem.at[step]))
        loads[-1].start()

    barrier = pltpu.get_barrier_semaphore()

    def greet_y(step, carry):
        pl.semaphore_signal(barrier, inc=1, device_id=(lax.rem(me_y + step, ny), me_z), device_id_type=MESH)
        return carry

    def greet_z(step, carry):
        pl.semaphore_signal(barrier, inc=1, device_id=(me_y, lax.rem(me_z + step, nz)), device_id_type=MESH)
        return carry

    lax.fori_loop(1, ny, greet_y, 0)
    lax.fori_loop(1, nz, greet_z, 0)

    groups = chunk_rows // 8
    for step, chunk in enumerate(order):
        loads[step].wait()

        def add_rows(group, carry):
            group = chunk * groups + group
            added = cells[pl.ds(group * 8, 8)].sum(axis=1)
            first, last = added[:, :128], added[:, 128:]
            side_part[2 * group] = jnp.concatenate([first[:4], last[:4]], axis=0)
            side_part[2 * group + 1] = jnp.concatenate([first[4:], last[4:]], axis=0)
            return carry

        lax.fori_loop(0, groups, add_rows, 0, unroll=True)
        if step == 0:
            pl.semaphore_wait(barrier, ny - 1 + nz - 1)

        def send(turn, carry):
            to = chunk * span + lax.rem(me_y + turn, span)

            @pl.when(to != me_y)
            def _():
                pltpu.make_async_remote_copy(
                    src_ref=side_part.at[to],
                    dst_ref=side_recv.at[me_y],
                    send_sem=send_sem.at[0],
                    recv_sem=recv_sem.at[0],
                    device_id=(to, me_z),
                    device_id_type=MESH,
                ).start()

            return carry

        lax.fori_loop(0, span, send, 0)

    side_recv[me_y] = side_part[me_y]

    ones = jnp.ones((width, 128), jnp.bfloat16)
    lane = iota(1)

    def add_columns(owner, carry):
        block = jnp.zeros((8, 128), jnp.float32)
        for k in range(8):
            piece = cells[pl.ds(owner * 64 + 8 * k, 8)].reshape(8 * depth, width)
            high = piece.astype(jnp.bfloat16)
            low = (piece - high.astype(jnp.float32)).astype(jnp.bfloat16)
            added = jnp.dot(high, ones, preferred_element_type=jnp.float32)
            added += jnp.dot(low, ones, preferred_element_type=jnp.float32)
            for x in range(8):
                for half in range(2):
                    at = 16 * x + 8 * half
                    block = jnp.where(lane == 64 * half + 8 * k + x, added[at : at + 8], block)
        top_part[owner] = block
        return carry

    lax.fori_loop(0, nz, add_columns, 0)

    for turn in range(1, nz):
        to = lax.rem(me_z + turn, nz)
        pltpu.make_async_remote_copy(
            src_ref=top_part.at[to],
            dst_ref=top_recv.at[me_z],
            send_sem=send_sem.at[1],
            recv_sem=recv_sem.at[1],
            device_id=(me_y, to),
            device_id_type=MESH,
        ).start()
    top_recv[me_z] = top_part[me_z]

    def wait_all(ref, count, sem):
        held = ref.at[pl.ds(0, count)]
        pltpu.make_async_copy(held, held, sem).wait()

    next_y, last_y = lax.rem(me_y + 1, ny), lax.rem(me_y + ny - 1, ny)
    next_z, last_z = lax.rem(me_z + 1, nz), lax.rem(me_z + nz - 1, nz)
    peers = ((next_y, me_z), (last_y, me_z), (me_y, next_z), (me_y, last_z))

    def send_halo(source, halo, at):
        for slot, peer in enumerate(peers):
            pltpu.make_async_remote_copy(
                src_ref=source,
                dst_ref=halo.at[slot],
                send_sem=send_sem.at[at],
                recv_sem=recv_sem.at[at],
                device_id=peer,
                device_id_type=MESH,
            ).start()

    def edged(halo, slot, there):
        return jnp.where(there, halo[slot], 0.0)

    wait_all(side_recv, ny - 1, recv_sem.at[0])
    side_total = side_recv[...].sum(axis=0)
    wait_all(side_part, ny - 1, send_sem.at[0])
    side_part[0] = side_total
    send_halo(side_part.at[0], side_halo, 2)

    wait_all(top_recv, nz - 1, recv_sem.at[1])
    top_total = top_recv[...].sum(axis=0)
    wait_all(top_part, nz - 1, send_sem.at[1])
    top_part[0] = top_total
    send_halo(top_part.at[0], top_halo, 3)

    wait_all(side_halo, 4, recv_sem.at[2])
    maps = side_maps(
        side_total,
        edged(side_halo, 0, me_y > 0),
        edged(side_halo, 1, me_y < ny - 1),
        edged(side_halo, 2, me_z > 0),
        edged(side_halo, 3, me_z < nz - 1),
        y_factor,
    )
    for i, found in enumerate(maps):
        side_out[i, :, 0:128] = found[:4]
        side_out[i, :, 128:256] = found[4:]

    wait_all(top_halo, 4, recv_sem.at[3])
    maps = top_maps(
        top_total,
        edged(top_halo, 0, me_y > 0),
        edged(top_halo, 1, me_y < ny - 1),
        edged(top_halo, 2, me_z > 0),
        edged(top_halo, 3, me_z < nz - 1),
        z_factor,
    )
    for i, found in enumerate(maps):
        top_out[i, 0:8, :] = found[:, :64]
        top_out[i, 8:16, :] = found[:, 64:]

    wait_all(side_halo, 4, send_sem.at[2])
    wait_all(top_halo, 4, send_sem.at[3])


def solution(mesh):
    ny, nz = mesh.shape["gy"], mesh.shape["gz"]

    def body(density):
        rows, depth, width = density.shape
        call = pl.pallas_call(
            functools.partial(kernel, ny, nz, 1.0 / math.sqrt(depth * ny), 1.0 / math.sqrt(width * nz)),
            out_shape=(
                jax.ShapeDtypeStruct((3, rows // ny, width), jnp.float32),
                jax.ShapeDtypeStruct((3, depth, rows // nz), jnp.float32),
            ),
            in_specs=[pl.BlockSpec(memory_space=pl.ANY)],
            out_specs=(pl.BlockSpec(memory_space=pltpu.VMEM), pl.BlockSpec(memory_space=pltpu.VMEM)),
            scratch_shapes=[
                pltpu.VMEM((rows, depth, width), jnp.float32),
                pltpu.VMEM((ny, 8, 128), jnp.float32),
                pltpu.VMEM((ny, 8, 128), jnp.float32),
                pltpu.VMEM((4, 8, 128), jnp.float32),
                pltpu.VMEM((nz, 8, 128), jnp.float32),
                pltpu.VMEM((nz, 8, 128), jnp.float32),
                pltpu.VMEM((4, 8, 128), jnp.float32),
                pltpu.SemaphoreType.DMA((CHUNKS,)),
                pltpu.SemaphoreType.DMA((4,)),
                pltpu.SemaphoreType.DMA((4,)),
            ],
            compiler_params=pltpu.CompilerParams(
                collective_id=0, has_side_effects=True, vmem_limit_bytes=56 * 1024 * 1024
            ),
        )
        side, top = call(density)
        return side, jnp.swapaxes(top, 1, 2)

    return jax.shard_map(
        body,
        mesh=mesh,
        in_specs=(P(None, "gy", "gz"),),
        out_specs=(P(None, "gy", "gz"), P(None, "gz", "gy")),
        check_vma=False,
    )
```

```python
import functools
import math

import jax
import jax.numpy as jnp
from jax import lax
from jax.experimental import pallas as pl
from jax.experimental.pallas import tpu as pltpu
from jax.sharding import PartitionSpec as P

MESH = pl.DeviceIdType.MESH
CHUNKS = 8


def iota(axis):
    return lax.broadcasted_iota(jnp.int32, (8, 128), axis)


def side_maps(total, low_x, high_x, low_z, high_z, factor):
    row, lane = iota(0), iota(1)
    lower_x = jnp.where(row % 4 == 0, pltpu.roll(low_x, 5, 0), pltpu.roll(total, 1, 0))
    upper_x = jnp.where(row % 4 == 3, pltpu.roll(high_x, 3, 0), pltpu.roll(total, 7, 0))
    down = pltpu.roll(total, 1, 1)
    up = pltpu.roll(total, 127, 1)
    low_edge = pltpu.roll(jnp.where(row >= 4, low_z, total), 4, 0)
    high_edge = pltpu.roll(jnp.where(row < 4, high_z, total), 4, 0)
    lower_z = jnp.where(lane == 0, pltpu.roll(low_edge, 1, 1), down)
    upper_z = jnp.where(lane == 127, pltpu.roll(high_edge, 127, 1), up)
    grad_z = (upper_z - lower_z) * (0.5 * factor)
    grad_x = (upper_x - lower_x) * (0.5 * factor)
    curve = (upper_x + lower_x + upper_z + lower_z - 4.0 * total) * factor
    return grad_z, grad_x, curve


def top_maps(total, low_y, high_y, factor):
    row = iota(0)
    first, last = total
    lower_y = [pltpu.roll(jnp.where(row == 7, a, b), 1, 0) for a, b in ((low_y, first), (first, last))]
    upper_y = [pltpu.roll(jnp.where(row == 0, a, b), 7, 0) for a, b in ((last, first), (high_y, last))]
    for here, lower, upper in zip(total, lower_y, upper_y):
        lower_x, upper_x = pltpu.roll(here, 1, 1), pltpu.roll(here, 127, 1)
        yield (
            (upper - lower) * (0.5 * factor),
            (upper_x - lower_x) * (0.5 * factor),
            (upper_x + lower_x + upper + lower - 4.0 * here) * factor,
        )


def kernel(ny, nz, y_factor, z_factor, density, maps_out, cells, side_part, side_recv, side_total, side_halo, top_half,
           top_part, top_recv, top_total, top_halo, load_sem, send_sem, recv_sem, line_sem, side_sem, top_sem):
    rows, depth, width = cells.shape
    span = rows // CHUNKS
    owners = ny // CHUNKS
    me_y, me_z = lax.axis_index("gy"), lax.axis_index("gz")

    def load(j):
        at = pl.ds(j * span, span)
        return pltpu.make_async_copy(density.at[at], cells.at[at], load_sem.at[j])

    for j in range(CHUNKS):
        load(j).start()

    def remote(src, dst, send, recv, peer):
        return pltpu.make_async_remote_copy(
            src_ref=src, dst_ref=dst, send_sem=send, recv_sem=recv, device_id=peer, device_id_type=MESH
        )

    barrier = pltpu.get_barrier_semaphore()
    for to in range(ny):
        @pl.when(me_y != to)
        def _():
            pl.semaphore_signal(barrier, inc=1, device_id=(to, me_z), device_id_type=MESH)

    for z in range(1, nz):
        @pl.when(me_z < z)
        def _():
            pl.semaphore_signal(barrier, inc=1, device_id=(me_y, z), device_id_type=MESH)

    lane = iota(1)

    def add(j, carry):
        load(j).wait()
        block = jnp.zeros((8, 128), jnp.float32)
        place = lane - (j * span) % 64
        for k in range(span // 8):
            piece = cells[pl.ds(j * span + 8 * k, 8)]
            added = piece.sum(axis=1)
            first, last = added[:, :128], added[:, 128:]
            side_part[j * owners + 2 * k] = jnp.concatenate([first[:4], last[:4]], axis=0)
            side_part[j * owners + 2 * k + 1] = jnp.concatenate([first[4:], last[4:]], axis=0)
            added = (piece[:, :, :128] + piece[:, :, 128:]).sum(axis=2, keepdims=True)
            for x in range(8):
                for half in range(2):
                    here = added[x, 8 * half : 8 * half + 8]
                    block = jnp.where(place == 64 * half + 8 * k + x, here, block)
        top_half[j] = block
        return carry

    lax.fori_loop(0, CHUNKS, add, 0)

    pieces = CHUNKS // nz
    packed = []
    for z in range(nz):
        block = top_half[pieces * z]
        for i in range(1, pieces):
            block += top_half[pieces * z + i]
        packed.append(block)
    nothing = jnp.zeros((8, 128), jnp.float32)
    for z in range(nz):
        here = packed[z]
        above = packed[z + 1] if z + 1 < nz else nothing
        below = packed[z - 1] if z else nothing
        around = jnp.where(lane == 64, above, jnp.where(lane == 127, below, 0.0))
        turned = jnp.where(lane == 64, pltpu.roll(above, 64, 1), jnp.where(lane == 127, pltpu.roll(below, 64, 1), 0.0))
        top_part[z, 0] = jnp.where(lane < 64, here, turned)
        top_part[z, 1] = jnp.where(lane < 64, pltpu.roll(here, 64, 1), around)

    def send_top(z):
        remote(top_part.at[z], top_recv.at[me_z], send_sem.at[1], line_sem.at[me_z], (me_y, z)).start()

    def wait_top(z):
        pltpu.make_async_copy(top_recv.at[z], top_recv.at[z], line_sem.at[z]).wait()

    def wait_all(ref, count, sem):
        held = ref.at[pl.ds(0, count)]
        pltpu.make_async_copy(held, held, sem).wait()

    pl.semaphore_wait(barrier, ny - 1 + me_z)
    for z in range(nz - 1):
        @pl.when(me_z > z)
        def _():
            send_top(z)

    for to in range(ny):
        @pl.when(me_y != to)
        def _():
            remote(side_part.at[to], side_recv.at[me_y], send_sem.at[0], recv_sem.at[0], (to, me_z)).start()

    side_recv[me_y] = side_part[me_y]
    top_recv[me_z] = top_part[me_z]

    edges = (
        (me_y < ny - 1, (me_y + 1, me_z), me_y > 0),
        (me_y > 0, (me_y - 1, me_z), me_y < ny - 1),
        (me_z < nz - 1, (me_y, me_z + 1), me_z > 0),
        (me_z > 0, (me_y, me_z - 1), me_z < nz - 1),
    )

    def side_copy(slot):
        return remote(side_total, side_halo.at[slot], side_sem.at[slot], side_sem.at[4 + slot], edges[slot][1])

    def top_copy(slot):
        return remote(top_total.at[1 - slot], top_halo.at[slot], top_sem.at[slot], top_sem.at[2 + slot], edges[slot][1])

    def start(copy, slot):
        pl.when(edges[slot][0])(lambda: copy(slot).start())

    def wait_recv(copy, slot):
        pl.when(edges[slot][2])(lambda: copy(slot).wait_recv())

    def wait_send(copy, slot):
        pl.when(edges[slot][0])(lambda: copy(slot).wait_send())

    for slot, (_, _, receives) in enumerate(edges):
        @pl.when(jnp.logical_not(receives))
        def _():
            side_halo[slot] = nothing
            if slot < 2:
                top_halo[slot] = nothing

    wait_all(side_recv, ny - 1, recv_sem.at[0])
    side_sum = side_recv[...].sum(axis=0)
    side_total[...] = side_sum
    for slot in (3, 0, 1):
        start(side_copy, slot)

    for z in range(1, nz):
        @pl.when(me_z < z)
        def _():
            wait_top(z)
            send_top(z)

        pl.when(me_z + 1 == z)(lambda: side_copy(2).start())

    for z in range(nz - 1):
        @pl.when(me_z > z)
        def _():
            wait_top(z)

    top_sum = top_recv[...].sum(axis=0)
    top_total[...] = top_sum
    for slot in (0, 1):
        start(top_copy, slot)

    for slot in range(4):
        wait_recv(side_copy, slot)
    for i, found in enumerate(side_maps(side_sum, *(side_halo[i] for i in range(4)), y_factor)):
        maps_out[i] = found
    for slot in (0, 1):
        wait_recv(top_copy, slot)
    for half, maps in enumerate(top_maps((top_sum[0], top_sum[1]), top_halo[0], top_halo[1], z_factor)):
        for i, found in enumerate(maps):
            maps_out[3 + 2 * i + half] = found

    wait_all(side_recv, ny - 1, send_sem.at[0])
    wait_all(top_recv, nz - 1, send_sem.at[1])
    for slot in range(4):
        wait_send(side_copy, slot)
    for slot in (0, 1):
        wait_send(top_copy, slot)


def unpack(maps, side_out, top_out):
    for i in range(3):
        side_out[i, :, 0:128] = maps[i, :4]
        side_out[i, :, 128:256] = maps[i, 4:]
        top_out[i, 0:8, :] = maps[3 + 2 * i, :, :64]
        top_out[i, 8:16, :] = maps[4 + 2 * i, :, :64]


def solution(mesh):
    ny, nz = mesh.shape["gy"], mesh.shape["gz"]

    def body(density):
        rows, depth, width = density.shape

        def blocks(*count):
            return pltpu.VMEM((*count, 8, 128), jnp.float32)

        vmem = pl.BlockSpec(memory_space=pltpu.VMEM)
        maps = pl.pallas_call(
            functools.partial(kernel, ny, nz, 1.0 / math.sqrt(depth * ny), 1.0 / math.sqrt(width * nz)),
            out_shape=pltpu.VMEM((9, 8, 128), jnp.float32),
            in_specs=[pl.BlockSpec(memory_space=pltpu.HBM)],
            out_specs=vmem,
            scratch_shapes=[
                pltpu.VMEM((rows, depth, width), jnp.float32),
                blocks(ny),
                blocks(ny),
                blocks(),
                blocks(4),
                blocks(CHUNKS),
                blocks(nz, 2),
                blocks(nz, 2),
                blocks(2),
                blocks(2),
                pltpu.SemaphoreType.DMA((CHUNKS,)),
                pltpu.SemaphoreType.DMA((2,)),
                pltpu.SemaphoreType.DMA((1,)),
                pltpu.SemaphoreType.DMA((nz,)),
                pltpu.SemaphoreType.DMA((8,)),
                pltpu.SemaphoreType.DMA((4,)),
            ],
            compiler_params=pltpu.CompilerParams(
                collective_id=0, has_side_effects=True, vmem_limit_bytes=16 * 1024 * 1024
            ),
            name="views",
        )(pltpu.with_memory_space_constraint(density, pltpu.HBM))
        side, top = pl.pallas_call(
            unpack,
            out_shape=(
                jax.ShapeDtypeStruct((3, rows // ny, width), jnp.float32),
                jax.ShapeDtypeStruct((3, depth, rows // nz), jnp.float32),
            ),
            in_specs=[vmem],
            out_specs=(vmem, vmem),
            name="unpack",
        )(pltpu.with_memory_space_constraint(maps, pltpu.VMEM))
        return side, jnp.swapaxes(top, 1, 2)

    return jax.shard_map(
        body,
        mesh=mesh,
        in_specs=(P(None, "gy", "gz"),),
        out_specs=(P(None, "gy", "gz"), P(None, "gz", "gy")),
        check_vma=False,
    )
```

```python
import functools
import math

import jax
import jax.numpy as jnp
from jax import lax
from jax.experimental import pallas as pl
from jax.experimental.pallas import tpu as pltpu
from jax.sharding import PartitionSpec as P

MESH = pl.DeviceIdType.MESH
CHUNKS = 8


def iota(axis):
    return lax.broadcasted_iota(jnp.int32, (8, 128), axis)


def stencil(here, lower_a, upper_a, lower_x, upper_x, factor):
    return (
        (upper_a - lower_a) * (0.5 * factor),
        (upper_x - lower_x) * (0.5 * factor),
        (upper_x + lower_x + upper_a + lower_a - 4.0 * here) * factor,
    )


def side_maps(parts, low_x, high_x, low_z, high_z, factor):
    row, lane = iota(0), iota(1)
    around = (low_z, *parts, high_z)
    for h, here in enumerate(parts):
        yield stencil(
            here,
            pltpu.roll(jnp.where(lane == 127, around[h], here), 1, 1),
            pltpu.roll(jnp.where(lane == 0, around[h + 2], here), 127, 1),
            pltpu.roll(jnp.where(row == 7, low_x[h], here), 1, 0),
            pltpu.roll(jnp.where(row == 0, high_x[h], here), 7, 0),
            factor,
        )


def top_maps(parts, low_y, high_y, factor):
    row = iota(0)
    around = (low_y, *parts, high_y)
    for h, here in enumerate(parts):
        yield stencil(
            here,
            pltpu.roll(jnp.where(row == 7, around[h], here), 1, 0),
            pltpu.roll(jnp.where(row == 0, around[h + 2], here), 7, 0),
            pltpu.roll(here, 1, 1),
            pltpu.roll(here, 127, 1),
            factor,
        )


def kernel(ny, nz, y_factor, z_factor, density, maps_out, cells, side_part, side_mate, side_recv, side_total, side_halo,
           top_half, top_part, top_recv, top_total, top_halo, maps_mate, load_sem, mate_sem, side_sem, top_sem, halo_sem,
           maps_sem, ready_sem):
    rows, depth, width = cells.shape
    span = rows // CHUNKS
    chips = ny // 2
    me_y, me_z = lax.axis_index("gy"), lax.axis_index("gz")
    chip, core = me_y // 2, me_y % 2
    leads, follows = core == 1, core == 0
    lead, mate = (2 * chip + 1, me_z), (2 * chip, me_z)

    def load(j):
        at = pl.ds(j * span, span)
        return pltpu.make_async_copy(density.at[at], cells.at[at], load_sem.at[j])

    for j in range(CHUNKS):
        load(j).start()

    def remote(src, dst, send, recv, peer):
        return pltpu.make_async_remote_copy(
            src_ref=src, dst_ref=dst, send_sem=send, recv_sem=recv, device_id=peer, device_id_type=MESH
        )

    def signal(sem, peer):
        pl.semaphore_signal(sem, inc=1, device_id=peer, device_id_type=MESH)

    def wait_all(ref, sem):
        pltpu.make_async_copy(ref, ref, sem).wait()

    barrier = pltpu.get_barrier_semaphore()

    @pl.when(leads)
    def _():
        signal(barrier, mate)
        for n in range(chips):
            pl.when(chip != n)(lambda: signal(barrier, (2 * n + 1, me_z)))
        for z in range(1, nz):
            pl.when(me_z < z)(lambda: signal(barrier, (me_y, z)))

    @pl.when(follows)
    def _():
        pl.semaphore_wait(barrier, 1)

    lane = iota(1)

    def add(j, carry):
        load(j).wait()
        block = jnp.zeros((8, 128), jnp.float32)
        place = lane - (j * span) % 64
        for k in range(span // 8):
            piece = cells[pl.ds(j * span + 8 * k, 8)]
            added = piece.sum(axis=1)
            side_part[j * (span // 8) + k, 0] = added[:, :128]
            side_part[j * (span // 8) + k, 1] = added[:, 128:]
            added = (piece[:, :, :128] + piece[:, :, 128:]).sum(axis=2, keepdims=True)
            for x in range(8):
                for half in range(2):
                    here = added[x, 8 * half : 8 * half + 8]
                    block = jnp.where(place == 64 * half + 8 * k + x, here, block)
        top_half[j] = block

        @pl.when(follows)
        def _():
            at = pl.ds(j * (span // 8), span // 8)
            remote(side_part.at[at], side_mate.at[at], mate_sem.at[0], mate_sem.at[1], lead).start()

        return carry

    lax.fori_loop(0, CHUNKS, add, 0)

    pieces = CHUNKS // nz
    packed = []
    for z in range(nz):
        block = top_half[pieces * z]
        for i in range(1, pieces):
            block += top_half[pieces * z + i]
        packed.append(block)
    nothing = jnp.zeros((8, 128), jnp.float32)
    for z in range(nz):
        here = packed[z]
        above = packed[z + 1] if z + 1 < nz else nothing
        below = packed[z - 1] if z else nothing
        around = jnp.where(lane == 64, above, jnp.where(lane == 127, below, 0.0))
        turned = jnp.where(lane == 64, pltpu.roll(above, 64, 1), jnp.where(lane == 127, pltpu.roll(below, 64, 1), 0.0))
        top_part[core, z, 0] = jnp.where(lane < 64, here, turned)
        top_part[core, z, 1] = jnp.where(lane < 64, pltpu.roll(here, 64, 1), around)

    @pl.when(follows)
    def _():
        remote(top_part.at[0], top_part.at[0], mate_sem.at[2], mate_sem.at[3], lead).start()
        wait_all(side_part, mate_sem.at[0])
        wait_all(top_part.at[0], mate_sem.at[2])
        wait_all(maps_out.at[pl.ds(0, 6)], maps_sem.at[2])
        wait_all(maps_out.at[pl.ds(6, 6)], maps_sem.at[3])

    @pl.when(leads)
    def _():
        edges = (
            (chip < chips - 1, (me_y + 2, me_z), chip > 0),
            (chip > 0, (me_y - 2, me_z), chip < chips - 1),
            (me_z < nz - 1, (me_y, me_z + 1), me_z > 0),
            (me_z > 0, (me_y, me_z - 1), me_z < nz - 1),
        )

        def halo(slot):
            if slot < 2:
                src, dst = side_total, side_halo.at[slot]
            elif slot < 4:
                src, dst = side_total.at[3 - slot], side_halo.at[2, slot - 2]
            else:
                src, dst = top_total.at[3 * (5 - slot)], top_halo.at[slot - 4]
            return remote(src, dst, halo_sem.at[slot], halo_sem.at[6 + slot], edges[slot % 4][1])

        def start(slot):
            pl.when(edges[slot % 4][0])(lambda: halo(slot).start())

        def wait_recv(slot):
            pl.when(edges[slot % 4][2])(lambda: halo(slot).wait_recv())

        def wait_send(slot):
            pl.when(edges[slot % 4][0])(lambda: halo(slot).wait_send())

        def send_top(z):
            for c in range(2):
                remote(top_part.at[c, z], top_recv.at[me_z, c], top_sem.at[0], top_sem.at[1], (me_y, z)).start()

        @pl.when(jnp.logical_not(edges[0][2]))
        def _():
            side_halo[0] = jnp.zeros((2, 8, 128), jnp.float32)
            top_halo[0] = nothing

        @pl.when(jnp.logical_not(edges[1][2]))
        def _():
            side_halo[1] = jnp.zeros((2, 8, 128), jnp.float32)
            top_halo[1] = nothing

        @pl.when(jnp.logical_not(edges[2][2]))
        def _():
            side_halo[2, 0] = nothing

        @pl.when(jnp.logical_not(edges[3][2]))
        def _():
            side_halo[2, 1] = nothing

        pl.semaphore_wait(barrier, chips - 1 + me_z)
        for z in range(nz - 1):
            pl.when(me_z > z)(lambda: signal(ready_sem.at[me_z], (me_y, z)))
        wait_all(top_part.at[0], mate_sem.at[3])
        for z in range(nz - 1):
            pl.when(me_z > z)(lambda: send_top(z))
        wait_all(side_mate, mate_sem.at[1])
        side_part[...] += side_mate[...]
        for n in range(chips):
            @pl.when(chip != n)
            def _():
                remote(side_part.at[n], side_recv.at[chip], side_sem.at[0], side_sem.at[1], (2 * n + 1, me_z)).start()

        side_recv[chip] = side_part[chip]
        top_recv[me_z, 0] = top_part[0, me_z]
        top_recv[me_z, 1] = top_part[1, me_z]

        wait_all(side_recv.at[pl.ds(0, chips - 1)], side_sem.at[1])
        side_total[...] = side_recv[...].sum(axis=0)
        for slot in (3, 0, 1):
            start(slot)
        for z in range(1, nz):
            @pl.when(me_z < z)
            def _():
                pl.semaphore_wait(ready_sem.at[z], 1)
                send_top(z)

            pl.when(me_z + 1 == z)(lambda: halo(2).start())

        wait_all(top_recv.at[pl.ds(0, nz - 1)], top_sem.at[1])
        top_total[...] = top_recv[...].sum(axis=0).reshape(4, 8, 128)
        for slot in (4, 5):
            start(slot)

        for slot in range(4):
            wait_recv(slot)
        parts = [side_total[h] for h in range(2)]
        found = side_maps(
            parts,
            [side_halo[0, h] for h in range(2)],
            [side_halo[1, h] for h in range(2)],
            side_halo[2, 0],
            side_halo[2, 1],
            y_factor,
        )
        for h, maps in enumerate(found):
            for i in range(3):
                maps_mate[2 * i + h] = maps[i]
                maps_out[2 * i + h] = pltpu.roll(maps[i], 4, 0)
        at = pl.ds(0, 6)
        remote(maps_mate.at[at], maps_out.at[at], maps_sem.at[0], maps_sem.at[2], mate).start()

        for slot in (4, 5):
            wait_recv(slot)
        parts = [top_total[h] for h in range(4)]
        for h, maps in enumerate(top_maps(parts, top_halo[0], top_halo[1], z_factor)):
            for i in range(3):
                (maps_out if h // 2 else maps_mate)[6 + 2 * i + h % 2] = maps[i]
        at = pl.ds(6, 6)
        remote(maps_mate.at[at], maps_out.at[at], maps_sem.at[1], maps_sem.at[3], mate).start()

        wait_all(side_recv.at[pl.ds(0, chips - 1)], side_sem.at[0])
        wait_all(top_recv.at[pl.ds(0, nz - 1)], top_sem.at[0])
        for slot in range(6):
            wait_send(slot)
        wait_all(maps_mate.at[pl.ds(0, 6)], maps_sem.at[0])
        wait_all(maps_mate.at[pl.ds(6, 6)], maps_sem.at[1])


def unpack(maps, side_out, top_out):
    for i in range(3):
        side_out[i, :, 0:128] = maps[2 * i, :4]
        side_out[i, :, 128:256] = maps[2 * i + 1, :4]
        top_out[i, 0:8, :] = maps[6 + 2 * i, :, :64]
        top_out[i, 8:16, :] = maps[7 + 2 * i, :, :64]


def solution(mesh):
    ny, nz = mesh.shape["gy"], mesh.shape["gz"]
    chips = ny // 2

    def body(density):
        rows, depth, width = density.shape

        def blocks(*count):
            return pltpu.VMEM((*count, 8, 128), jnp.float32)

        vmem = pl.BlockSpec(memory_space=pltpu.VMEM)
        maps = pl.pallas_call(
            functools.partial(kernel, ny, nz, 1.0 / math.sqrt(depth * ny), 1.0 / math.sqrt(width * nz)),
            out_shape=pltpu.VMEM((12, 8, 128), jnp.float32),
            in_specs=[pl.BlockSpec(memory_space=pltpu.HBM)],
            out_specs=vmem,
            scratch_shapes=[
                pltpu.VMEM((rows, depth, width), jnp.float32),
                blocks(chips, 2),
                blocks(chips, 2),
                blocks(chips, 2),
                blocks(2),
                blocks(3, 2),
                blocks(CHUNKS),
                blocks(2, nz, 2),
                blocks(nz, 2, 2),
                blocks(4),
                blocks(2),
                blocks(12),
                pltpu.SemaphoreType.DMA((CHUNKS,)),
                pltpu.SemaphoreType.DMA((4,)),
                pltpu.SemaphoreType.DMA((2,)),
                pltpu.SemaphoreType.DMA((2,)),
                pltpu.SemaphoreType.DMA((12,)),
                pltpu.SemaphoreType.DMA((4,)),
                pltpu.SemaphoreType.REGULAR((nz,)),
            ],
            compiler_params=pltpu.CompilerParams(
                collective_id=0, has_side_effects=True, vmem_limit_bytes=16 * 1024 * 1024
            ),
            name="views",
        )(pltpu.with_memory_space_constraint(density, pltpu.HBM))
        side, top = pl.pallas_call(
            unpack,
            out_shape=(
                jax.ShapeDtypeStruct((3, rows // ny, width), jnp.float32),
                jax.ShapeDtypeStruct((3, depth, rows // nz), jnp.float32),
            ),
            in_specs=[vmem],
            out_specs=(vmem, vmem),
            name="unpack",
        )(pltpu.with_memory_space_constraint(maps, pltpu.VMEM))
        return side, jnp.swapaxes(top, 1, 2)

    return jax.shard_map(
        body,
        mesh=mesh,
        in_specs=(P(None, "gy", "gz"),),
        out_specs=(P(None, "gy", "gz"), P(None, "gz", "gy")),
        check_vma=False,
    )
```

```python
import functools
import math

import jax
import jax.numpy as jnp
from jax import lax
from jax.experimental import pallas as pl
from jax.experimental.pallas import tpu as pltpu
from jax.sharding import PartitionSpec as P

MESH = pl.DeviceIdType.MESH
CHUNKS = 8


def iota(axis):
    return lax.broadcasted_iota(jnp.int32, (8, 128), axis)


def stencil(here, lower_a, upper_a, lower_x, upper_x, factor):
    return (
        (upper_a - lower_a) * (0.5 * factor),
        (upper_x - lower_x) * (0.5 * factor),
        (upper_x + lower_x + upper_a + lower_a - 4.0 * here) * factor,
    )


def side_maps(parts, low_x, high_x, low_z, high_z, factor):
    row, lane = iota(0), iota(1)
    around = (low_z, *parts, high_z)
    for h, here in enumerate(parts):
        yield stencil(
            here,
            pltpu.roll(jnp.where(lane == 127, around[h], here), 1, 1),
            pltpu.roll(jnp.where(lane == 0, around[h + 2], here), 127, 1),
            pltpu.roll(jnp.where(row == 7, low_x[h], here), 1, 0),
            pltpu.roll(jnp.where(row == 0, high_x[h], here), 7, 0),
            factor,
        )


def top_maps(parts, low_y, high_y, factor):
    row = iota(0)
    around = (low_y, *parts, high_y)
    for h, here in enumerate(parts):
        yield stencil(
            here,
            pltpu.roll(jnp.where(row == 7, around[h], here), 1, 0),
            pltpu.roll(jnp.where(row == 0, around[h + 2], here), 7, 0),
            pltpu.roll(here, 1, 1),
            pltpu.roll(here, 127, 1),
            factor,
        )


def kernel(ny, nz, y_factor, z_factor, density, maps_out, cells, side_part, side_mate, side_recv, side_total, side_halo,
           top_half, top_part, top_recv, top_total, top_halo, maps_mate, load_sem, mate_sem, side_sem, top_sem, halo_sem,
           maps_sem, chunk_sem, line_sem, ready_sem):
    rows, depth, width = cells.shape
    span = rows // CHUNKS
    chips = ny // 2
    me_y, me_z = lax.axis_index("gy"), lax.axis_index("gz")
    chip, core = me_y // 2, me_y % 2
    leads, follows = core == 1, core == 0
    lead, mate = (2 * chip + 1, me_z), (2 * chip, me_z)

    def load(j):
        at = pl.ds(j * span, span)
        return pltpu.make_async_copy(density.at[at], cells.at[at], load_sem.at[j])

    for j in range(CHUNKS):
        load(j).start()

    def remote(src, dst, send, recv, peer):
        return pltpu.make_async_remote_copy(
            src_ref=src, dst_ref=dst, send_sem=send, recv_sem=recv, device_id=peer, device_id_type=MESH
        )

    def signal(sem, peer):
        pl.semaphore_signal(sem, inc=1, device_id=peer, device_id_type=MESH)

    def wait_all(ref, sem):
        pltpu.make_async_copy(ref, ref, sem).wait()

    barrier = pltpu.get_barrier_semaphore()

    @pl.when(leads)
    def _():
        signal(barrier, mate)
        for n in range(chips):
            pl.when(chip != n)(lambda: signal(barrier, (2 * n + 1, me_z)))

    for z in range(1, nz):
        pl.when(me_z < z)(lambda: signal(barrier, (2 * chip, z)))

    lane = iota(1)

    def add(j, carry):
        load(j).wait()
        block = jnp.zeros((8, 128), jnp.float32)
        place = lane - (j * span) % 64
        for k in range(span // 8):
            piece = cells[pl.ds(j * span + 8 * k, 8)]
            added = piece.sum(axis=1)
            side_part[j * (span // 8) + k, 0] = added[:, :128]
            side_part[j * (span // 8) + k, 1] = added[:, 128:]
            added = (piece[:, :, :128] + piece[:, :, 128:]).sum(axis=2, keepdims=True)
            for x in range(8):
                for half in range(2):
                    here = added[x, 8 * half : 8 * half + 8]
                    block = jnp.where(place == 64 * half + 8 * k + x, here, block)
        top_half[j] = block

        return carry

    owners = span // 8

    def hand_over(j, carry):
        at = pl.ds(j * owners, owners)
        remote(side_part.at[at], side_mate.at[at], mate_sem.at[0], chunk_sem.at[j], lead).start()
        return carry

    def send_side(j, carry):
        at = pl.ds(j * owners, owners)
        wait_all(side_mate.at[at], chunk_sem.at[j])
        side_part[at] += side_mate[at]
        for q in range(owners):
            n = j * owners + q

            @pl.when(chip != n)
            def _():
                remote(side_part.at[n], side_recv.at[chip], side_sem.at[0], side_sem.at[1], (2 * n + 1, me_z)).start()

        return carry

    @pl.when(follows)
    def _():
        add(0, 0)
        pl.semaphore_wait(barrier, 1 + 2 * me_z)
        signal(line_sem, lead)
        hand_over(0, 0)
        for z in range(nz - 1):
            @pl.when(me_z > z)
            def _():
                signal(ready_sem.at[me_z], (2 * chip + 1, z))
                signal(ready_sem.at[me_z], (2 * chip, z))

        lax.fori_loop(1, CHUNKS, lambda j, carry: hand_over(j, add(j, carry)), 0)

    @pl.when(leads)
    def _():
        lax.fori_loop(0, CHUNKS, add, 0)
        pl.semaphore_wait(line_sem, 1)

    pieces = CHUNKS // nz
    packed = []
    for z in range(nz):
        block = top_half[pieces * z]
        for i in range(1, pieces):
            block += top_half[pieces * z + i]
        packed.append(block)
    nothing = jnp.zeros((8, 128), jnp.float32)
    for z in range(nz):
        here = packed[z]
        above = packed[z + 1] if z + 1 < nz else nothing
        below = packed[z - 1] if z else nothing
        around = jnp.where(lane == 64, above, jnp.where(lane == 127, below, 0.0))
        turned = jnp.where(lane == 64, pltpu.roll(above, 64, 1), jnp.where(lane == 127, pltpu.roll(below, 64, 1), 0.0))
        top_part[z, 0] = jnp.where(lane < 64, here, turned)
        top_part[z, 1] = jnp.where(lane < 64, pltpu.roll(here, 64, 1), around)

    def send_top(z):
        peer = (2 * chip + 1, z)
        remote(top_part.at[z], top_recv.at[2 * me_z + core], top_sem.at[0], top_sem.at[1], peer).start()

    def send_up():
        for z in range(1, nz):
            @pl.when(me_z < z)
            def _():
                pl.semaphore_wait(ready_sem.at[z], 1)
                send_top(z)

    for z in range(nz - 1):
        pl.when(me_z > z)(lambda: send_top(z))

    @pl.when(follows)
    def _():
        send_top(me_z)
        send_up()
        wait_all(side_part, mate_sem.at[0])
        wait_all(top_part, top_sem.at[0])
        wait_all(maps_out.at[pl.ds(0, 6)], maps_sem.at[2])
        wait_all(maps_out.at[pl.ds(6, 6)], maps_sem.at[3])

    @pl.when(leads)
    def _():
        edges = (
            (chip < chips - 1, (me_y + 2, me_z), chip > 0),
            (chip > 0, (me_y - 2, me_z), chip < chips - 1),
            (me_z < nz - 1, (me_y, me_z + 1), me_z > 0),
            (me_z > 0, (me_y, me_z - 1), me_z < nz - 1),
        )

        def halo(slot):
            if slot < 2:
                src, dst = side_total, side_halo.at[slot]
            elif slot < 4:
                src, dst = side_total.at[3 - slot], side_halo.at[2, slot - 2]
            else:
                src, dst = top_total.at[3 * (5 - slot)], top_halo.at[slot - 4]
            return remote(src, dst, halo_sem.at[slot], halo_sem.at[6 + slot], edges[slot % 4][1])

        def start(slot):
            pl.when(edges[slot % 4][0])(lambda: halo(slot).start())

        def wait_recv(slot):
            pl.when(edges[slot % 4][2])(lambda: halo(slot).wait_recv())

        def wait_send(slot):
            pl.when(edges[slot % 4][0])(lambda: halo(slot).wait_send())

        @pl.when(jnp.logical_not(edges[0][2]))
        def _():
            side_halo[0] = jnp.zeros((2, 8, 128), jnp.float32)
            top_halo[0] = nothing

        @pl.when(jnp.logical_not(edges[1][2]))
        def _():
            side_halo[1] = jnp.zeros((2, 8, 128), jnp.float32)
            top_halo[1] = nothing

        @pl.when(jnp.logical_not(edges[2][2]))
        def _():
            side_halo[2, 0] = nothing

        @pl.when(jnp.logical_not(edges[3][2]))
        def _():
            side_halo[2, 1] = nothing

        pl.semaphore_wait(barrier, chips - 1)
        lax.fori_loop(0, CHUNKS, send_side, 0)
        send_up()
        side_recv[chip] = side_part[chip]
        top_recv[2 * me_z + 1] = top_part[me_z]

        wait_all(side_recv.at[pl.ds(0, chips - 1)], side_sem.at[1])
        side_total[...] = side_recv[...].sum(axis=0)
        for slot in (3, 0, 1, 2):
            start(slot)
        wait_all(top_recv.at[pl.ds(0, 2 * nz - 1)], top_sem.at[1])
        for h in range(4):
            added = top_recv[h // 2, h % 2]
            for z in range(1, nz):
                added += top_recv[2 * z + h // 2, h % 2]
            top_total[h] = added
        for slot in (4, 5):
            start(slot)

        for slot in range(4):
            wait_recv(slot)
        parts = [side_total[h] for h in range(2)]
        found = side_maps(
            parts,
            [side_halo[0, h] for h in range(2)],
            [side_halo[1, h] for h in range(2)],
            side_halo[2, 0],
            side_halo[2, 1],
            y_factor,
        )
        for h, maps in enumerate(found):
            for i in range(3):
                maps_mate[2 * i + h] = maps[i]
                maps_out[2 * i + h] = pltpu.roll(maps[i], 4, 0)
        at = pl.ds(0, 6)
        remote(maps_mate.at[at], maps_out.at[at], maps_sem.at[0], maps_sem.at[2], mate).start()

        for slot in (4, 5):
            wait_recv(slot)
        parts = [top_total[h] for h in range(4)]
        for h, maps in enumerate(top_maps(parts, top_halo[0], top_halo[1], z_factor)):
            for i in range(3):
                (maps_out if h // 2 else maps_mate)[6 + 2 * i + h % 2] = maps[i]
        at = pl.ds(6, 6)
        remote(maps_mate.at[at], maps_out.at[at], maps_sem.at[1], maps_sem.at[3], mate).start()

        wait_all(side_recv.at[pl.ds(0, chips - 1)], side_sem.at[0])
        wait_all(top_part.at[pl.ds(0, nz - 1)], top_sem.at[0])
        for slot in range(6):
            wait_send(slot)
        wait_all(maps_mate.at[pl.ds(0, 6)], maps_sem.at[0])
        wait_all(maps_mate.at[pl.ds(6, 6)], maps_sem.at[1])


def unpack(maps, side_out, top_out):
    for i in range(3):
        side_out[i, :, 0:128] = maps[2 * i, :4]
        side_out[i, :, 128:256] = maps[2 * i + 1, :4]
        top_out[i, 0:8, :] = maps[6 + 2 * i, :, :64]
        top_out[i, 8:16, :] = maps[7 + 2 * i, :, :64]


def solution(mesh):
    ny, nz = mesh.shape["gy"], mesh.shape["gz"]
    chips = ny // 2

    def body(density):
        rows, depth, width = density.shape

        def blocks(*count):
            return pltpu.VMEM((*count, 8, 128), jnp.float32)

        vmem = pl.BlockSpec(memory_space=pltpu.VMEM)
        maps = pl.pallas_call(
            functools.partial(kernel, ny, nz, 1.0 / math.sqrt(depth * ny), 1.0 / math.sqrt(width * nz)),
            out_shape=pltpu.VMEM((12, 8, 128), jnp.float32),
            in_specs=[pl.BlockSpec(memory_space=pltpu.HBM)],
            out_specs=vmem,
            scratch_shapes=[
                pltpu.VMEM((rows, depth, width), jnp.float32),
                blocks(chips, 2),
                blocks(chips, 2),
                blocks(chips, 2),
                blocks(2),
                blocks(3, 2),
                blocks(CHUNKS),
                blocks(nz, 2),
                blocks(2 * nz, 2),
                blocks(4),
                blocks(2),
                blocks(12),
                pltpu.SemaphoreType.DMA((CHUNKS,)),
                pltpu.SemaphoreType.DMA((1,)),
                pltpu.SemaphoreType.DMA((2,)),
                pltpu.SemaphoreType.DMA((2,)),
                pltpu.SemaphoreType.DMA((12,)),
                pltpu.SemaphoreType.DMA((4,)),
                pltpu.SemaphoreType.DMA((CHUNKS,)),
                pltpu.SemaphoreType.REGULAR,
                pltpu.SemaphoreType.REGULAR((nz,)),
            ],
            compiler_params=pltpu.CompilerParams(
                collective_id=0, has_side_effects=True, vmem_limit_bytes=16 * 1024 * 1024
            ),
            name="views",
        )(pltpu.with_memory_space_constraint(density, pltpu.HBM))
        side, top = pl.pallas_call(
            unpack,
            out_shape=(
                jax.ShapeDtypeStruct((3, rows // ny, width), jnp.float32),
                jax.ShapeDtypeStruct((3, depth, rows // nz), jnp.float32),
            ),
            in_specs=[vmem],
            out_specs=(vmem, vmem),
            name="unpack",
        )(pltpu.with_memory_space_constraint(maps, pltpu.VMEM))
        return side, jnp.swapaxes(top, 1, 2)

    return jax.shard_map(
        body,
        mesh=mesh,
        in_specs=(P(None, "gy", "gz"),),
        out_specs=(P(None, "gy", "gz"), P(None, "gz", "gy")),
        check_vma=False,
    )
```

```python
import functools
import math

import jax
import jax.numpy as jnp
from jax import lax
from jax.experimental import pallas as pl
from jax.experimental.pallas import tpu as pltpu
from jax.sharding import PartitionSpec as P

MESH = pl.DeviceIdType.MESH
CHUNKS = 8


def iota(axis):
    return lax.broadcasted_iota(jnp.int32, (8, 128), axis)


def stencil(here, lower_a, upper_a, lower_x, upper_x, factor):
    return (
        (upper_a - lower_a) * (0.5 * factor),
        (upper_x - lower_x) * (0.5 * factor),
        (upper_x + lower_x + upper_a + lower_a - 4.0 * here) * factor,
    )


def side_maps(parts, low_x, high_x, low_z, high_z, factor):
    row, lane = iota(0), iota(1)
    around = (low_z, *parts, high_z)
    for h, here in enumerate(parts):
        yield stencil(
            here,
            pltpu.roll(jnp.where(lane == 127, around[h], here), 1, 1),
            pltpu.roll(jnp.where(lane == 0, around[h + 2], here), 127, 1),
            pltpu.roll(jnp.where(row == 7, low_x[h], here), 1, 0),
            pltpu.roll(jnp.where(row == 0, high_x[h], here), 7, 0),
            factor,
        )


def top_maps(below, parts, above, factor):
    row = iota(0)
    around = (below, *parts, above)
    for h, here in enumerate(parts):
        yield stencil(
            here,
            pltpu.roll(jnp.where(row == 7, around[h], here), 1, 0),
            pltpu.roll(jnp.where(row == 0, around[h + 2], here), 7, 0),
            pltpu.roll(here, 1, 1),
            pltpu.roll(here, 127, 1),
            factor,
        )


def kernel(ny, nz, y_factor, z_factor, density, maps_out, cells, side_part, side_mate, side_recv, side_total, side_halo,
           top_half, top_part, top_recv, top_total, top_halo, load_sem, mate_sem, side_sem, top_sem, edge_sem, chunk_sem,
           line_sem, ready_sem):
    rows, depth, width = cells.shape
    span = rows // CHUNKS
    chips = ny // 2
    me_y, me_z = lax.axis_index("gy"), lax.axis_index("gz")
    chip, core = me_y // 2, me_y % 2
    leads, follows = core == 1, core == 0
    lead, mate = (2 * chip + 1, me_z), (2 * chip, me_z)

    def load(j):
        at = pl.ds(j * span, span)
        return pltpu.make_async_copy(density.at[at], cells.at[at], load_sem.at[j])

    for j in range(CHUNKS):
        load(j).start()

    def remote(src, dst, send, recv, peer):
        return pltpu.make_async_remote_copy(
            src_ref=src, dst_ref=dst, send_sem=send, recv_sem=recv, device_id=peer, device_id_type=MESH
        )

    def signal(sem, peer):
        pl.semaphore_signal(sem, inc=1, device_id=peer, device_id_type=MESH)

    def wait_all(ref, sem):
        pltpu.make_async_copy(ref, ref, sem).wait()

    barrier = pltpu.get_barrier_semaphore()

    @pl.when(leads)
    def _():
        signal(barrier, mate)
        for n in range(chips):
            pl.when(chip != n)(lambda: signal(barrier, (2 * n + 1, me_z)))

    for z in range(1, nz):
        pl.when(me_z < z)(lambda: signal(barrier, (2 * chip, z)))

    lane = iota(1)

    def add(j, carry):
        load(j).wait()
        block = jnp.zeros((8, 128), jnp.float32)
        place = lane - (j * span) % 64
        for k in range(span // 8):
            piece = cells[pl.ds(j * span + 8 * k, 8)]
            added = piece.sum(axis=1)
            side_part[j * (span // 8) + k, 0] = added[:, :128]
            side_part[j * (span // 8) + k, 1] = added[:, 128:]
            added = (piece[:, :, :128] + piece[:, :, 128:]).sum(axis=2, keepdims=True)
            for x in range(8):
                for half in range(2):
                    here = added[x, 8 * half : 8 * half + 8]
                    block = jnp.where(place == 64 * half + 8 * k + x, here, block)
        top_half[j] = block

        return carry

    owners = span // 8

    def hand_over(j, carry):
        at = pl.ds(j * owners, owners)
        remote(side_part.at[at], side_mate.at[at], mate_sem.at[0], chunk_sem.at[j], lead).start()
        return carry

    def send_side(j, carry):
        at = pl.ds(j * owners, owners)
        wait_all(side_mate.at[at], chunk_sem.at[j])
        side_part[at] += side_mate[at]
        for q in range(owners):
            n = j * owners + q

            @pl.when(chip != n)
            def _():
                remote(side_part.at[n], side_recv.at[chip], side_sem.at[0], side_sem.at[1], (2 * n + 1, me_z)).start()

        return carry

    @pl.when(follows)
    def _():
        add(0, 0)
        pl.semaphore_wait(barrier, 1 + 2 * me_z)
        signal(line_sem, lead)
        hand_over(0, 0)
        for z in range(nz - 1):
            @pl.when(me_z > z)
            def _():
                signal(ready_sem.at[me_z], (2 * chip + 1, z))
                signal(ready_sem.at[me_z], (2 * chip, z))

        lax.fori_loop(1, CHUNKS, lambda j, carry: hand_over(j, add(j, carry)), 0)

    @pl.when(leads)
    def _():
        lax.fori_loop(0, CHUNKS, add, 0)
        pl.semaphore_wait(line_sem, 1)

    pieces = CHUNKS // nz
    packed = []
    for z in range(nz):
        block = top_half[pieces * z]
        for i in range(1, pieces):
            block += top_half[pieces * z + i]
        packed.append(block)
    nothing = jnp.zeros((8, 128), jnp.float32)
    for z in range(nz):
        here = packed[z]
        above = packed[z + 1] if z + 1 < nz else nothing
        below = packed[z - 1] if z else nothing
        around = jnp.where(lane == 64, above, jnp.where(lane == 127, below, 0.0))
        turned = jnp.where(lane == 64, pltpu.roll(above, 64, 1), jnp.where(lane == 127, pltpu.roll(below, 64, 1), 0.0))
        top_part[z, 0] = jnp.where(lane < 64, here, turned)
        top_part[z, 1] = jnp.where(lane < 64, pltpu.roll(here, 64, 1), around)

    def send_top(z):
        peer = (2 * chip + 1, z)
        remote(top_part.at[z], top_recv.at[2 * me_z + core], top_sem.at[0], top_sem.at[1], peer).start()

    def send_up():
        for z in range(1, nz):
            @pl.when(me_z < z)
            def _():
                pl.semaphore_wait(ready_sem.at[z], 1)
                send_top(z)

    for z in range(nz - 1):
        pl.when(me_z > z)(lambda: send_top(z))

    up, down = 2 * chip + 3, 2 * chip - 1
    totals = (
        (side_total, side_halo.at[0], chip < chips - 1, chip > 0, (up - 1, me_z)),
        (side_total, side_halo.at[0], chip > 0, chip < chips - 1, (down, me_z)),
        (side_total.at[1], side_halo.at[1, 0], me_z < nz - 1, me_z > 0, (me_y, me_z + 1)),
        (side_total.at[0], side_halo.at[1, 1], me_z > 0, me_z < nz - 1, (me_y, me_z - 1)),
        (side_total.at[1], side_halo.at[1, 0], me_z < nz - 1, me_z > 0, (2 * chip, me_z + 1)),
        (side_total.at[0], side_halo.at[1, 1], me_z > 0, me_z < nz - 1, (2 * chip, me_z - 1)),
        (side_total, side_total, leads, follows, mate),
        (top_total.at[3], top_halo, chip < chips - 1, chip > 0, (up - 1, me_z)),
        (top_total.at[0], top_halo, chip > 0, chip < chips - 1, (down, me_z)),
        (top_total, top_total, leads, follows, mate),
    )

    def total(k):
        src, dst, _, _, peer = totals[k]
        return remote(src, dst, edge_sem.at[k], edge_sem.at[len(totals) + k], peer)

    def send_totals(*which):
        for k in which:
            pl.when(totals[k][2])(lambda: total(k).start())

    def wait_totals(*which):
        for k in which:
            pl.when(totals[k][3])(lambda: total(k).wait_recv())

    for h, missing in enumerate((me_z == 0, me_z == nz - 1)):
        @pl.when(missing)
        def _():
            side_halo[1, h] = nothing

    @pl.when(me_y % (ny - 1) == 0)
    def _():
        side_halo[0] = jnp.zeros((2, 8, 128), jnp.float32)
        top_halo[...] = nothing

    def make_side(shift):
        beside = [side_halo[0, h] for h in range(2)]
        parts = [side_total[h] for h in range(2)]
        for h, maps in enumerate(side_maps(parts, beside, beside, side_halo[1, 0], side_halo[1, 1], y_factor)):
            for i in range(3):
                maps_out[2 * i + h] = pltpu.roll(maps[i], 4, 0) if shift else maps[i]

    def make_top(below, parts, above):
        for h, maps in enumerate(top_maps(below, parts, above, z_factor)):
            for i in range(3):
                maps_out[6 + 2 * i + h] = maps[i]

    @pl.when(follows)
    def _():
        send_top(me_z)
        send_up()
        wait_all(side_part, mate_sem.at[0])
        wait_all(top_part, top_sem.at[0])
        wait_totals(6, 0, 4, 5)
        make_side(False)
        wait_totals(9, 7)
        make_top(top_halo[...], [top_total[0], top_total[1]], top_total[2])

    @pl.when(leads)
    def _():
        pl.semaphore_wait(barrier, chips - 1)
        lax.fori_loop(0, CHUNKS, send_side, 0)
        send_up()
        side_recv[chip] = side_part[chip]
        top_recv[2 * me_z + 1] = top_part[me_z]

        wait_all(side_recv.at[pl.ds(0, chips - 1)], side_sem.at[1])
        side_total[...] = side_recv[...].sum(axis=0)
        send_totals(3, 5, 2, 4, 1, 0, 6)

        wait_all(top_recv.at[pl.ds(0, 2 * nz - 1)], top_sem.at[1])
        for h in range(4):
            added = top_recv[h // 2, h % 2]
            for z in range(1, nz):
                added += top_recv[2 * z + h // 2, h % 2]
            top_total[h] = added
        send_totals(8, 7, 9)

        wait_all(side_recv.at[pl.ds(0, chips - 1)], side_sem.at[0])
        wait_all(top_part.at[pl.ds(0, nz - 1)], top_sem.at[0])
        wait_totals(1, 2, 3)
        make_side(True)
        wait_totals(8)
        make_top(top_total[1], [top_total[2], top_total[3]], top_halo[...])
        for k in range(len(totals)):
            pl.when(totals[k][2])(lambda: total(k).wait_send())


def unpack(maps, side_out, top_out):
    for i in range(3):
        side_out[i, :, 0:128] = maps[2 * i, :4]
        side_out[i, :, 128:256] = maps[2 * i + 1, :4]
        top_out[i, 0:8, :] = maps[6 + 2 * i, :, :64]
        top_out[i, 8:16, :] = maps[7 + 2 * i, :, :64]


def solution(mesh):
    ny, nz = mesh.shape["gy"], mesh.shape["gz"]
    chips = ny // 2

    def body(density):
        rows, depth, width = density.shape

        def blocks(*count):
            return pltpu.VMEM((*count, 8, 128), jnp.float32)

        vmem = pl.BlockSpec(memory_space=pltpu.VMEM)
        maps = pl.pallas_call(
            functools.partial(kernel, ny, nz, 1.0 / math.sqrt(depth * ny), 1.0 / math.sqrt(width * nz)),
            out_shape=pltpu.VMEM((12, 8, 128), jnp.float32),
            in_specs=[pl.BlockSpec(memory_space=pltpu.HBM)],
            out_specs=vmem,
            scratch_shapes=[
                pltpu.VMEM((rows, depth, width), jnp.float32),
                blocks(chips, 2),
                blocks(chips, 2),
                blocks(chips, 2),
                blocks(2),
                blocks(2, 2),
                blocks(CHUNKS),
                blocks(nz, 2),
                blocks(2 * nz, 2),
                blocks(4),
                blocks(),
                pltpu.SemaphoreType.DMA((CHUNKS,)),
                pltpu.SemaphoreType.DMA((1,)),
                pltpu.SemaphoreType.DMA((2,)),
                pltpu.SemaphoreType.DMA((2,)),
                pltpu.SemaphoreType.DMA((20,)),
                pltpu.SemaphoreType.DMA((CHUNKS,)),
                pltpu.SemaphoreType.REGULAR,
                pltpu.SemaphoreType.REGULAR((nz,)),
            ],
            compiler_params=pltpu.CompilerParams(
                collective_id=0, has_side_effects=True, vmem_limit_bytes=16 * 1024 * 1024
            ),
            name="views",
        )(pltpu.with_memory_space_constraint(density, pltpu.HBM))
        side, top = pl.pallas_call(
            unpack,
            out_shape=(
                jax.ShapeDtypeStruct((3, rows // ny, width), jnp.float32),
                jax.ShapeDtypeStruct((3, depth, rows // nz), jnp.float32),
            ),
            in_specs=[vmem],
            out_specs=(vmem, vmem),
            name="unpack",
        )(pltpu.with_memory_space_constraint(maps, pltpu.VMEM))
        return side, jnp.swapaxes(top, 1, 2)

    return jax.shard_map(
        body,
        mesh=mesh,
        in_specs=(P(None, "gy", "gz"),),
        out_specs=(P(None, "gy", "gz"), P(None, "gz", "gy")),
        check_vma=False,
    )
```

```python
import functools
import math

import jax
import jax.numpy as jnp
from jax import lax
from jax.experimental import pallas as pl
from jax.experimental.pallas import tpu as pltpu
from jax.sharding import PartitionSpec as P

MESH = pl.DeviceIdType.MESH
CHUNKS = 8
LOADS = 8


def iota(axis):
    return lax.broadcasted_iota(jnp.int32, (8, 128), axis)


def stencil(here, lower_a, upper_a, lower_x, upper_x, factor):
    return (
        (upper_a - lower_a) * (0.5 * factor),
        (upper_x - lower_x) * (0.5 * factor),
        (upper_x + lower_x + upper_a + lower_a - 4.0 * here) * factor,
    )


def side_maps(parts, low_x, high_x, low_z, high_z, factor):
    row, lane = iota(0), iota(1)
    around = (low_z, *parts, high_z)
    for h, here in enumerate(parts):
        yield stencil(
            here,
            pltpu.roll(jnp.where(lane == 127, around[h], here), 1, 1),
            pltpu.roll(jnp.where(lane == 0, around[h + 2], here), 127, 1),
            pltpu.roll(jnp.where(row == 7, low_x[h], here), 1, 0),
            pltpu.roll(jnp.where(row == 0, high_x[h], here), 7, 0),
            factor,
        )


def top_maps(below, parts, above, factor):
    row = iota(0)
    around = (below, *parts, above)
    for h, here in enumerate(parts):
        yield stencil(
            here,
            pltpu.roll(jnp.where(row == 7, around[h], here), 1, 0),
            pltpu.roll(jnp.where(row == 0, around[h + 2], here), 7, 0),
            pltpu.roll(here, 1, 1),
            pltpu.roll(here, 127, 1),
            factor,
        )


def kernel(ny, nz, y_factor, z_factor, density, maps_out, cells, side_part, side_mate, side_recv, side_total, side_halo,
           top_half, top_part, top_recv, top_total, top_halo, load_sem, chunk_sem, out_sem, side_sem, top_sem, edge_out,
           edge_in, line_sem, ready_sem):
    rows, depth, width = cells.shape
    span = rows // CHUNKS
    chips = ny // 2
    tiles = depth * width // 1024
    me_y, me_z = lax.axis_index("gy"), lax.axis_index("gz")
    chip, core = me_y // 2, me_y % 2
    leads, follows = core == 1, core == 0
    lead, mate = (2 * chip + 1, me_z), (2 * chip, me_z)

    def load(i):
        at = pl.ds(i * (rows // LOADS), rows // LOADS)
        return pltpu.make_async_copy(density.at[at], cells.at[at], load_sem.at[i])

    for i in range(LOADS):
        load(i).start()

    def remote(src, dst, send, recv, peer):
        return pltpu.make_async_remote_copy(
            src_ref=src, dst_ref=dst, send_sem=send, recv_sem=recv, device_id=peer, device_id_type=MESH
        )

    def signal(sem, peer):
        pl.semaphore_signal(sem, inc=1, device_id=peer, device_id_type=MESH)

    def wait_all(ref, sem):
        pltpu.make_async_copy(ref, ref, sem).wait()

    barrier = pltpu.get_barrier_semaphore()

    @pl.when(leads)
    def _():
        signal(barrier, mate)
        for n in range(chips):
            pl.when(chip != n)(lambda: signal(barrier, (2 * n + 1, me_z)))

    for z in range(1, nz):
        pl.when(me_z < z)(lambda: signal(barrier, (2 * chip, z)))

    lane = iota(1)

    def add(j):
        pl.when(j % (CHUNKS // LOADS) == 0)(lambda: load(j // (CHUNKS // LOADS)).wait())
        block = jnp.zeros((8, 128), jnp.float32)
        place = lane - (j * span) % 64
        for k in range(span // 8):
            piece = cells[pl.ds(j * span + 8 * k, 8)]
            added = piece.sum(axis=1)
            side_part[j * (span // 8) + k, 0] = added[:, :128]
            side_part[j * (span // 8) + k, 1] = added[:, 128:]
            added = (piece[:, :, :128] + piece[:, :, 128:]).sum(axis=2, keepdims=True)
            for x in range(8):
                for half in range(2):
                    here = added[x, 8 * half : 8 * half + 8]
                    block = jnp.where(place == 64 * half + 8 * k + x, here, block)
        top_half[j] = block


    owners = span // 8
    nothing = jnp.zeros((8, 128), jnp.float32)

    def hand_over(j):
        at = pl.ds(j * owners, owners)
        remote(side_part.at[at], side_mate.at[at], out_sem, chunk_sem.at[(j + 3) // 4], lead).start()

    def send_side(j, carry):
        for lot, first, end in ((0, 0, 1), (1, 1, 5), (2, 5, CHUNKS)):
            pl.when(j == first)(
                lambda: wait_all(side_mate.at[pl.ds(first * owners, (end - first) * owners)], chunk_sem.at[lot])
            )
        at = pl.ds(j * owners, owners)
        side_part[at] += side_mate[at]
        for q in range(owners):
            n = j * owners + q

            @pl.when(chip != n)
            def _():
                remote(side_part.at[n], side_recv.at[chip], out_sem, side_sem, (2 * n + 1, me_z)).start()

        return carry

    def send_top(z):
        remote(top_part.at[z], top_recv.at[2 * me_z + core], out_sem, top_sem, (2 * chip + 1, z)).start()

    def pack(z, above):
        here = top_half[2 * z] + top_half[2 * z + 1]
        below = jnp.where(z > 0, top_half[jnp.maximum(2 * z - 1, 0)], 0.0)
        around = jnp.where(lane == 64, above, jnp.where(lane == 127, below, 0.0))
        turned = jnp.where(lane == 64, pltpu.roll(above, 64, 1), jnp.where(lane == 127, pltpu.roll(below, 64, 1), 0.0))
        top_part[z, 0] = jnp.where(lane < 64, here, turned)
        top_part[z, 1] = jnp.where(lane < 64, pltpu.roll(here, 64, 1), around)

    def step(j, carry):
        add(j)

        @pl.when(follows)
        def _():
            @pl.when(j == 0)
            def _():
                pl.semaphore_wait(barrier, 1 + 2 * me_z)
                signal(line_sem, lead)

            hand_over(j)

            @pl.when(j == 0)
            def _():
                for z in range(nz - 1):
                    @pl.when(me_z > z)
                    def _():
                        signal(ready_sem, (2 * chip + 1, z))
                        signal(ready_sem, (2 * chip, z))

        @pl.when(jnp.logical_and(j >= 2, j % 2 == 0))
        def _():
            z = j // 2 - 1
            pack(z, top_half[j])
            pl.when(jnp.logical_and(leads, z == 0))(lambda: pl.semaphore_wait(line_sem, 1))
            pl.when(z < me_z)(lambda: send_top(z))

        return carry

    lax.fori_loop(0, CHUNKS - 1, step, 0)

    @pl.when(leads)
    def _():
        pl.semaphore_wait(barrier, chips - 1)
        lax.fori_loop(0, 2, send_side, 0)

    lax.fori_loop(CHUNKS - 1, CHUNKS, step, 0)

    def send_up():
        pl.when(me_z < nz - 1)(lambda: pl.semaphore_wait(ready_sem, nz - 1 - me_z))
        for z in range(1, nz):
            pl.when(me_z < z)(lambda: send_top(z))

    up, down = 2 * chip + 3, 2 * chip - 1
    last, top = chip == chips - 1, me_z == nz - 1
    totals = (
        (side_total, side_halo.at[0], ~last, chip > 0, (up - 1, me_z), 0, edge_in.at[0]),
        (side_total, side_halo.at[0], chip > 0, ~last, (down, me_z), 1, edge_in.at[0]),
        (side_total.at[1], side_halo.at[1, 0], ~top, me_z > 0, (me_y, me_z + 1), 2, edge_in.at[1]),
        (side_total.at[0], side_halo.at[1, 1], me_z > 0, ~top, (me_y, me_z - 1), 3, edge_in.at[2]),
        (side_total.at[1], side_halo.at[1, 0], ~top, me_z > 0, (2 * chip, me_z + 1), 2, edge_in.at[1]),
        (side_total.at[0], side_halo.at[1, 1], me_z > 0, ~top, (2 * chip, me_z - 1), 3, edge_in.at[2]),
        (side_total, side_total, leads, follows, mate, 4, side_sem),
        (top_total.at[3], top_halo, ~last, chip > 0, (up - 1, me_z), 0, edge_in.at[3]),
        (top_total.at[0], top_halo, chip > 0, ~last, (down, me_z), 1, edge_in.at[3]),
        (top_total, top_total, leads, follows, mate, 4, top_sem),
    )

    def total(k):
        src, dst, _, _, peer, send, recv = totals[k]
        return remote(src, dst, edge_out.at[send], recv, peer)

    def send_totals(*which):
        for k in which:
            pl.when(totals[k][2])(lambda: total(k).start())

    def wait_totals(*which):
        for k in which:
            pl.when(totals[k][3])(lambda: total(k).wait_recv())

    for h, missing in enumerate((me_z == 0, me_z == nz - 1)):
        @pl.when(missing)
        def _():
            side_halo[1, h] = nothing

    @pl.when(me_y % (ny - 1) == 0)
    def _():
        side_halo[0] = jnp.zeros((2, 8, 128), jnp.float32)
        top_halo[...] = nothing

    def make_side(shift):
        beside = [side_halo[0, h] for h in range(2)]
        parts = [side_total[h] for h in range(2)]
        for h, maps in enumerate(side_maps(parts, beside, beside, side_halo[1, 0], side_halo[1, 1], y_factor)):
            for i in range(3):
                maps_out[2 * i + h] = pltpu.roll(maps[i], 4, 0) if shift else maps[i]

    def make_top(below, parts, above):
        for h, maps in enumerate(top_maps(below, parts, above, z_factor)):
            for i in range(3):
                maps_out[6 + 2 * i + h] = maps[i]

    @pl.when(follows)
    def _():
        pack(nz - 1, nothing)
        send_top(me_z)
        send_up()
        wait_totals(6, 0, 4, 5)
        make_side(False)
        wait_totals(9, 7)
        make_top(top_halo[...], [top_total[0], top_total[1]], top_total[2])
        wait_all(cells.at[pl.ds(0, (2 * chips + 2 * nz) // tiles)], out_sem)

    @pl.when(leads)
    def _():
        lax.fori_loop(2, CHUNKS, send_side, 0)
        pack(nz - 1, nothing)
        send_up()
        side_recv[chip] = side_part[chip]
        top_recv[2 * me_z + 1] = top_part[me_z]

        wait_all(side_recv.at[pl.ds(0, chips - 1)], side_sem)
        side_total[...] = side_recv[...].sum(axis=0)
        send_totals(3, 5, 2, 4, 1, 0, 6)

        wait_all(top_recv.at[pl.ds(0, 2 * nz - 1)], top_sem)
        for h in range(4):
            added = top_recv[h // 2, h % 2]
            for z in range(1, nz):
                added += top_recv[2 * z + h // 2, h % 2]
            top_total[h] = added
        send_totals(8, 7, 9)

        wait_all(cells.at[pl.ds(0, (2 * (chips - 1) + 2 * (nz - 1)) // tiles)], out_sem)
        wait_totals(8)
        make_top(top_total[1], [top_total[2], top_total[3]], top_halo[...])
        for send, (out, count) in enumerate(((~last, 3), (chip > 0, 3), (~top, 2), (me_z > 0, 2))):
            pl.when(out)(lambda: wait_all(top_total.at[pl.ds(0, count)], edge_out.at[send]))
        wait_all(top_part.at[pl.ds(0, 3)], edge_out.at[4])
        wait_totals(1, 2, 3)
        make_side(True)


def unpack(maps, side_out, top_out):
    for i in range(3):
        side_out[i, :, 0:128] = maps[2 * i, :4]
        side_out[i, :, 128:256] = maps[2 * i + 1, :4]
        top_out[i, 0:8, :] = maps[6 + 2 * i, :, :64]
        top_out[i, 8:16, :] = maps[7 + 2 * i, :, :64]


def solution(mesh):
    ny, nz = mesh.shape["gy"], mesh.shape["gz"]
    chips = ny // 2

    def body(density):
        rows, depth, width = density.shape

        def blocks(*count):
            return pltpu.VMEM((*count, 8, 128), jnp.float32)

        vmem = pl.BlockSpec(memory_space=pltpu.VMEM)
        maps = pl.pallas_call(
            functools.partial(kernel, ny, nz, 1.0 / math.sqrt(depth * ny), 1.0 / math.sqrt(width * nz)),
            out_shape=pltpu.VMEM((12, 8, 128), jnp.float32),
            in_specs=[pl.BlockSpec(memory_space=pltpu.HBM)],
            out_specs=vmem,
            scratch_shapes=[
                pltpu.VMEM((rows, depth, width), jnp.float32),
                blocks(chips, 2),
                blocks(chips, 2),
                blocks(chips, 2),
                blocks(2),
                blocks(2, 2),
                blocks(CHUNKS),
                blocks(nz, 2),
                blocks(2 * nz, 2),
                blocks(4),
                blocks(),
                pltpu.SemaphoreType.DMA((LOADS,)),
                pltpu.SemaphoreType.DMA((3,)),
                pltpu.SemaphoreType.DMA,
                pltpu.SemaphoreType.DMA,
                pltpu.SemaphoreType.DMA,
                pltpu.SemaphoreType.DMA((5,)),
                pltpu.SemaphoreType.DMA((4,)),
                pltpu.SemaphoreType.REGULAR,
                pltpu.SemaphoreType.REGULAR,
            ],
            compiler_params=pltpu.CompilerParams(
                collective_id=0, has_side_effects=True, vmem_limit_bytes=16 * 1024 * 1024
            ),
            name="views",
        )(pltpu.with_memory_space_constraint(density, pltpu.HBM))
        side, top = pl.pallas_call(
            unpack,
            out_shape=(
                jax.ShapeDtypeStruct((3, rows // ny, width), jnp.float32),
                jax.ShapeDtypeStruct((3, depth, rows // nz), jnp.float32),
            ),
            in_specs=[vmem],
            out_specs=(vmem, vmem),
            name="unpack",
        )(pltpu.with_memory_space_constraint(maps, pltpu.VMEM))
        return side, jnp.swapaxes(top, 1, 2)

    return jax.shard_map(
        body,
        mesh=mesh,
        in_specs=(P(None, "gy", "gz"),),
        out_specs=(P(None, "gy", "gz"), P(None, "gz", "gy")),
        check_vma=False,
    )
```

```python
import functools
import math

import jax
import jax.numpy as jnp
from jax import lax
from jax.experimental import pallas as pl
from jax.experimental.pallas import tpu as pltpu
from jax.sharding import PartitionSpec as P

MESH = pl.DeviceIdType.MESH
CHUNKS = 8
LOADS = 8


def iota(axis):
    return lax.broadcasted_iota(jnp.int32, (8, 128), axis)


def stencil(here, lower_a, upper_a, lower_x, upper_x, factor):
    return (
        (upper_a - lower_a) * (0.5 * factor),
        (upper_x - lower_x) * (0.5 * factor),
        (upper_x + lower_x + upper_a + lower_a - 4.0 * here) * factor,
    )


def side_maps(parts, low_x, high_x, low_z, high_z, factor):
    row, lane = iota(0), iota(1)
    around = (low_z, *parts, high_z)
    for h, here in enumerate(parts):
        yield stencil(
            here,
            pltpu.roll(jnp.where(lane == 127, around[h], here), 1, 1),
            pltpu.roll(jnp.where(lane == 0, around[h + 2], here), 127, 1),
            pltpu.roll(jnp.where(row == 7, low_x[h], here), 1, 0),
            pltpu.roll(jnp.where(row == 0, high_x[h], here), 7, 0),
            factor,
        )


def top_maps(below, parts, above, factor):
    row = iota(0)
    around = (below, *parts, above)
    for h, here in enumerate(parts):
        yield stencil(
            here,
            pltpu.roll(jnp.where(row == 7, around[h], here), 1, 0),
            pltpu.roll(jnp.where(row == 0, around[h + 2], here), 7, 0),
            pltpu.roll(here, 1, 1),
            pltpu.roll(here, 127, 1),
            factor,
        )


def kernel(ny, nz, y_factor, z_factor, density, maps_out, cells, side_part, side_mate, side_recv, side_total, side_halo, side_low, side_high, edge_part, edge_recv,
           top_half, top_part, top_recv, top_total, top_halo, load_sem, chunk_sem, out_sem, side_sem, top_sem, edge_out,
           edge_in, line_sem, ready_sem):
    rows, depth, width = cells.shape
    span = rows // CHUNKS
    chips = ny // 2
    tiles = depth * width // 1024
    me_y, me_z = lax.axis_index("gy"), lax.axis_index("gz")
    chip, core = me_y // 2, me_y % 2
    leads, follows = core == 1, core == 0
    lead, mate = (2 * chip + 1, me_z), (2 * chip, me_z)

    def load(i):
        at = pl.ds(i * (rows // LOADS), rows // LOADS)
        return pltpu.make_async_copy(density.at[at], cells.at[at], load_sem.at[i])

    for i in range(LOADS):
        load(i).start()

    def remote(src, dst, send, recv, peer):
        return pltpu.make_async_remote_copy(
            src_ref=src, dst_ref=dst, send_sem=send, recv_sem=recv, device_id=peer, device_id_type=MESH
        )

    def signal(sem, peer):
        pl.semaphore_signal(sem, inc=1, device_id=peer, device_id_type=MESH)

    def wait_all(ref, sem):
        pltpu.make_async_copy(ref, ref, sem).wait()

    barrier = pltpu.get_barrier_semaphore()

    @pl.when(leads)
    def _():
        signal(barrier, mate)
        for n in range(chips):
            pl.when(chip != n)(lambda: signal(barrier, (2 * n + 1, me_z)))

        @pl.when(me_z < nz - 1)
        def _():
            for n in range(chips):
                signal(barrier, (2 * n + 1, me_z + 1))

    for z in range(1, nz):
        pl.when(me_z < z)(lambda: signal(barrier, (2 * chip, z)))

    lane = iota(1)

    def add(j):
        pl.when(j % (CHUNKS // LOADS) == 0)(lambda: load(j // (CHUNKS // LOADS)).wait())
        block = jnp.zeros((8, 128), jnp.float32)
        place = lane - (j * span) % 64
        for k in range(span // 8):
            piece = cells[pl.ds(j * span + 8 * k, 8)]
            added = piece.sum(axis=1)
            side_part[j * (span // 8) + k, 0] = added[:, :128]
            side_part[j * (span // 8) + k, 1] = added[:, 128:]
            added = (piece[:, :, :128] + piece[:, :, 128:]).sum(axis=2, keepdims=True)
            for x in range(8):
                for half in range(2):
                    here = added[x, 8 * half : 8 * half + 8]
                    block = jnp.where(place == 64 * half + 8 * k + x, here, block)
        top_half[j] = block


    owners = span // 8
    nothing = jnp.zeros((8, 128), jnp.float32)

    def hand_over(j):
        at = pl.ds(j * owners, owners)
        remote(side_part.at[at], side_mate.at[at], out_sem, chunk_sem.at[(j + 3) // 4], lead).start()

    def send_side(j, carry):
        for lot, first, end in ((0, 0, 1), (1, 1, 5), (2, 5, CHUNKS)):
            pl.when(j == first)(
                lambda: wait_all(side_mate.at[pl.ds(first * owners, (end - first) * owners)], chunk_sem.at[lot])
            )
        at = pl.ds(j * owners, owners)
        side_part[at] += side_mate[at]
        @pl.when(me_z > 0)
        def _():
            columns = jnp.broadcast_to(side_part[at, 0][:, :, :1], (owners, 8, 128))
            edge_part[at, 0:1] = jnp.where((iota(0) == lane)[None], columns, 0.0).sum(axis=1, keepdims=True)
            for q in range(owners):
                n = j * owners + q
                src, dst = edge_part.at[n, pl.ds(0, 1)], edge_recv.at[chip, pl.ds(0, 1)]
                remote(src, dst, out_sem, edge_in.at[2], (2 * n + 1, me_z - 1)).start()

        for q in range(owners):
            n = j * owners + q

            @pl.when(chip != n)
            def _():
                remote(side_part.at[n], side_recv.at[chip], out_sem, side_sem, (2 * n + 1, me_z)).start()

        return carry

    def send_top(z):
        remote(top_part.at[z], top_recv.at[2 * me_z + core], out_sem, top_sem, (2 * chip + 1, z)).start()

    def pack(z, above):
        here = top_half[2 * z] + top_half[2 * z + 1]
        below = jnp.where(z > 0, top_half[jnp.maximum(2 * z - 1, 0)], 0.0)
        around = jnp.where(lane == 64, above, jnp.where(lane == 127, below, 0.0))
        turned = jnp.where(lane == 64, pltpu.roll(above, 64, 1), jnp.where(lane == 127, pltpu.roll(below, 64, 1), 0.0))
        top_part[z, 0] = jnp.where(lane < 64, here, turned)
        top_part[z, 1] = jnp.where(lane < 64, pltpu.roll(here, 64, 1), around)

    def step(j, carry):
        add(j)

        @pl.when(follows)
        def _():
            @pl.when(j == 0)
            def _():
                pl.semaphore_wait(barrier, 1 + 2 * me_z)
                signal(line_sem, lead)

            hand_over(j)

            @pl.when(j == 0)
            def _():
                for z in range(nz - 1):
                    @pl.when(me_z > z)
                    def _():
                        signal(ready_sem, (2 * chip + 1, z))
                        signal(ready_sem, (2 * chip, z))

        @pl.when(jnp.logical_and(j >= 2, j % 2 == 0))
        def _():
            z = j // 2 - 1
            pack(z, top_half[j])
            pl.when(jnp.logical_and(leads, z == 0))(lambda: pl.semaphore_wait(line_sem, 1))
            pl.when(z < me_z)(lambda: send_top(z))

        return carry

    lax.fori_loop(0, CHUNKS - 1, step, 0)

    @pl.when(leads)
    def _():
        pl.when(me_z == 0)(lambda: pl.semaphore_wait(barrier, chips - 1))
        pl.when(me_z > 0)(lambda: pl.semaphore_wait(barrier, 2 * chips - 1))
        lax.fori_loop(0, 2, send_side, 0)

    lax.fori_loop(CHUNKS - 1, CHUNKS, step, 0)

    def send_up():
        pl.when(me_z < nz - 1)(lambda: pl.semaphore_wait(ready_sem, nz - 1 - me_z))
        for z in range(1, nz):
            pl.when(me_z < z)(lambda: send_top(z))

    up, down = 2 * chip + 3, 2 * chip - 1
    last, top = chip == chips - 1, me_z == nz - 1
    totals = (
        (side_total, side_halo, ~last, chip > 0, (up - 1, me_z), 0, edge_in.at[0]),
        (side_total, side_halo, chip > 0, ~last, (down, me_z), 1, edge_in.at[0]),
        (side_total.at[1], side_low, ~top, me_z > 0, (me_y, me_z + 1), 2, edge_in.at[1]),
        (side_total.at[1], side_low, ~top, me_z > 0, (2 * chip, me_z + 1), 2, edge_in.at[1]),
        (side_high, side_high, ~top, ~top, mate, 3, edge_in.at[2]),
        (side_total, side_total, leads, follows, mate, 4, side_sem),
        (top_total.at[3], top_halo, ~last, chip > 0, (up - 1, me_z), 0, edge_in.at[3]),
        (top_total.at[0], top_halo, chip > 0, ~last, (down, me_z), 1, edge_in.at[3]),
        (top_total, top_total, leads, follows, mate, 4, top_sem),
    )

    def total(k):
        src, dst, _, _, peer, send, recv = totals[k]
        return remote(src, dst, edge_out.at[send], recv, peer)

    def send_totals(*which):
        for k in which:
            pl.when(totals[k][2])(lambda: total(k).start())

    def wait_totals(*which):
        for k in which:
            pl.when(totals[k][3])(lambda: total(k).wait_recv())

    @pl.when(me_z == 0)
    def _():
        side_low[...] = nothing

    @pl.when(top)
    def _():
        side_high[...] = nothing

    @pl.when(me_y % (ny - 1) == 0)
    def _():
        side_halo[...] = jnp.zeros((2, 8, 128), jnp.float32)
        top_halo[...] = nothing

    def make_side(shift):
        beside = [side_halo[h] for h in range(2)]
        parts = [side_total[h] for h in range(2)]
        for h, maps in enumerate(side_maps(parts, beside, beside, side_low[...], side_high[...], y_factor)):
            for i in range(3):
                maps_out[2 * i + h] = pltpu.roll(maps[i], 4, 0) if shift else maps[i]

    def make_top(below, parts, above):
        for h, maps in enumerate(top_maps(below, parts, above, z_factor)):
            for i in range(3):
                maps_out[6 + 2 * i + h] = maps[i]

    @pl.when(follows)
    def _():
        pack(nz - 1, nothing)
        send_top(me_z)
        send_up()
        wait_totals(8, 6)
        make_top(top_halo[...], [top_total[0], top_total[1]], top_total[2])
        wait_totals(5, 0, 3, 4)
        make_side(False)
        wait_all(cells.at[pl.ds(0, (2 * chips + 2 * nz) // tiles)], out_sem)

    @pl.when(leads)
    def _():
        lax.fori_loop(2, CHUNKS, send_side, 0)
        pack(nz - 1, nothing)
        send_up()
        side_recv[chip] = side_part[chip]
        top_recv[2 * me_z + 1] = top_part[me_z]

        wait_all(side_recv.at[pl.ds(0, chips - 1)], side_sem)
        side_total[...] = side_recv[...].sum(axis=0)
        send_totals(2, 3, 1, 0, 5)

        wait_all(top_recv.at[pl.ds(0, 2 * nz - 1)], top_sem)
        for h in range(4):
            added = top_recv[h // 2, h % 2]
            for z in range(1, nz):
                added += top_recv[2 * z + h // 2, h % 2]
            top_total[h] = added
        send_totals(7, 6, 8)

        @pl.when(~top)
        def _():
            wait_all(edge_recv.at[pl.ds(0, chips), pl.ds(0, 1)], edge_in.at[2])
            column = jnp.broadcast_to(edge_recv[:, 0:1].sum(axis=0), (8, 128))
            column = jnp.where(iota(0) == lane, column, 0.0).sum(axis=1, keepdims=True)
            side_high[...] = jnp.broadcast_to(column, (8, 128))

        send_totals(4)
        sent = 2 * (chips - 1) + 2 * (nz - 1)
        pl.when(me_z == 0)(lambda: wait_all(cells.at[pl.ds(0, sent // tiles)], out_sem))
        pl.when(me_z > 0)(lambda: wait_all(cells.at[pl.ds(0, (sent + chips // 8) // tiles)], out_sem))
        wait_totals(7)
        make_top(top_total[1], [top_total[2], top_total[3]], top_halo[...])
        for send, (out, count) in enumerate(((~last, 3), (chip > 0, 3), (~top, 2))):
            pl.when(out)(lambda: wait_all(top_total.at[pl.ds(0, count)], edge_out.at[send]))
        wait_totals(1, 2)
        make_side(True)
        pl.when(~top)(lambda: wait_all(side_high, edge_out.at[3]))
        wait_all(top_part.at[pl.ds(0, 3)], edge_out.at[4])


def unpack(maps, side_out, top_out):
    for i in range(3):
        side_out[i, :, 0:128] = maps[2 * i, :4]
        side_out[i, :, 128:256] = maps[2 * i + 1, :4]
        top_out[i, 0:8, :] = maps[6 + 2 * i, :, :64]
        top_out[i, 8:16, :] = maps[7 + 2 * i, :, :64]


def solution(mesh):
    ny, nz = mesh.shape["gy"], mesh.shape["gz"]
    chips = ny // 2

    def body(density):
        rows, depth, width = density.shape

        def blocks(*count):
            return pltpu.VMEM((*count, 8, 128), jnp.float32)

        vmem = pl.BlockSpec(memory_space=pltpu.VMEM)
        maps = pl.pallas_call(
            functools.partial(kernel, ny, nz, 1.0 / math.sqrt(depth * ny), 1.0 / math.sqrt(width * nz)),
            out_shape=pltpu.VMEM((12, 8, 128), jnp.float32),
            in_specs=[pl.BlockSpec(memory_space=pltpu.HBM)],
            out_specs=vmem,
            scratch_shapes=[
                pltpu.VMEM((rows, depth, width), jnp.float32),
                blocks(chips, 2),
                blocks(chips, 2),
                blocks(chips, 2),
                blocks(2),
                blocks(2),
                blocks(),
                blocks(),
                blocks(chips),
                blocks(chips),
                blocks(CHUNKS),
                blocks(nz, 2),
                blocks(2 * nz, 2),
                blocks(4),
                blocks(),
                pltpu.SemaphoreType.DMA((LOADS,)),
                pltpu.SemaphoreType.DMA((3,)),
                pltpu.SemaphoreType.DMA,
                pltpu.SemaphoreType.DMA,
                pltpu.SemaphoreType.DMA,
                pltpu.SemaphoreType.DMA((5,)),
                pltpu.SemaphoreType.DMA((4,)),
                pltpu.SemaphoreType.REGULAR,
                pltpu.SemaphoreType.REGULAR,
            ],
            compiler_params=pltpu.CompilerParams(
                collective_id=0, has_side_effects=True, vmem_limit_bytes=16 * 1024 * 1024
            ),
            name="views",
        )(pltpu.with_memory_space_constraint(density, pltpu.HBM))
        side, top = pl.pallas_call(
            unpack,
            out_shape=(
                jax.ShapeDtypeStruct((3, rows // ny, width), jnp.float32),
                jax.ShapeDtypeStruct((3, depth, rows // nz), jnp.float32),
            ),
            in_specs=[vmem],
            out_specs=(vmem, vmem),
            name="unpack",
        )(pltpu.with_memory_space_constraint(maps, pltpu.VMEM))
        return side, jnp.swapaxes(top, 1, 2)

    return jax.shard_map(
        body,
        mesh=mesh,
        in_specs=(P(None, "gy", "gz"),),
        out_specs=(P(None, "gy", "gz"), P(None, "gz", "gy")),
        check_vma=False,
    )
```

```python
import functools
import math

import jax
import jax.numpy as jnp
from jax import lax
from jax.experimental import pallas as pl
from jax.experimental.pallas import tpu as pltpu
from jax.sharding import PartitionSpec as P

MESH = pl.DeviceIdType.MESH
CHUNKS = 8
LOADS = 8


def iota(axis):
    return lax.broadcasted_iota(jnp.int32, (8, 128), axis)


def stencil(here, lower_a, upper_a, lower_x, upper_x, factor):
    return (
        (upper_a - lower_a) * (0.5 * factor),
        (upper_x - lower_x) * (0.5 * factor),
        (upper_x + lower_x + upper_a + lower_a - 4.0 * here) * factor,
    )


def side_maps(parts, low_x, high_x, low_z, high_z, factor):
    row, lane = iota(0), iota(1)
    around = (low_z, *parts, high_z)
    for h, here in enumerate(parts):
        yield stencil(
            here,
            pltpu.roll(jnp.where(lane == 127, around[h], here), 1, 1),
            pltpu.roll(jnp.where(lane == 0, around[h + 2], here), 127, 1),
            pltpu.roll(jnp.where(row == 7, low_x[h], here), 1, 0),
            pltpu.roll(jnp.where(row == 0, high_x[h], here), 7, 0),
            factor,
        )


def top_maps(below, parts, above, factor):
    row = iota(0)
    around = (below, *parts, above)
    for h, here in enumerate(parts):
        yield stencil(
            here,
            pltpu.roll(jnp.where(row == 7, around[h], here), 1, 0),
            pltpu.roll(jnp.where(row == 0, around[h + 2], here), 7, 0),
            pltpu.roll(here, 1, 1),
            pltpu.roll(here, 127, 1),
            factor,
        )


def kernel(ny, nz, y_factor, z_factor, density, maps_out, cells, side_part, side_mate, side_recv, side_total, side_halo, side_low, side_high, side_next, edge_part, edge_recv,
           top_half, top_part, top_recv, top_total, top_halo, load_sem, chunk_sem, out_sem, side_sem, top_sem, edge_out,
           edge_in, line_sem, ready_sem):
    rows, depth, width = cells.shape
    span = rows // CHUNKS
    chips = ny // 2
    tiles = depth * width // 1024
    me_y, me_z = lax.axis_index("gy"), lax.axis_index("gz")
    chip, core = me_y // 2, me_y % 2
    leads, follows = core == 1, core == 0
    top = me_z == nz - 1
    rows_in, rows_out = me_z < nz // 2, (me_z > 0) & (me_z <= nz // 2)
    next_in, next_out = (me_z >= nz // 2) & ~top, me_z > nz // 2
    lead, mate = (2 * chip + 1, me_z), (2 * chip, me_z)

    def load(i):
        at = pl.ds(i * (rows // LOADS), rows // LOADS)
        return pltpu.make_async_copy(density.at[at], cells.at[at], load_sem.at[i])

    for i in range(LOADS):
        load(i).start()

    def remote(src, dst, send, recv, peer):
        return pltpu.make_async_remote_copy(
            src_ref=src, dst_ref=dst, send_sem=send, recv_sem=recv, device_id=peer, device_id_type=MESH
        )

    def signal(sem, peer):
        pl.semaphore_signal(sem, inc=1, device_id=peer, device_id_type=MESH)

    def wait_all(ref, sem):
        pltpu.make_async_copy(ref, ref, sem).wait()

    barrier = pltpu.get_barrier_semaphore()

    for z in range(1, nz):
        pl.when(me_z < z)(lambda: signal(barrier, (2 * chip, z)))

    @pl.when(leads)
    def _():
        signal(barrier, mate)
        for n in range(chips):
            pl.when(chip != n)(lambda: signal(barrier, (2 * n + 1, me_z)))

        @pl.when(rows_in)
        def _():
            for n in range(chips):
                signal(barrier, (2 * n + 1, me_z + 1))

    lane = iota(1)

    def add(j):
        pl.when(j % (CHUNKS // LOADS) == 0)(lambda: load(j // (CHUNKS // LOADS)).wait())
        block = jnp.zeros((8, 128), jnp.float32)
        place = lane - (j * span) % 64
        for k in range(span // 8):
            piece = cells[pl.ds(j * span + 8 * k, 8)]
            added = piece.sum(axis=1)
            side_part[j * (span // 8) + k, 0] = added[:, :128]
            side_part[j * (span // 8) + k, 1] = added[:, 128:]
            added = (piece[:, :, :128] + piece[:, :, 128:]).sum(axis=2, keepdims=True)
            for x in range(8):
                for half in range(2):
                    here = added[x, 8 * half : 8 * half + 8]
                    block = jnp.where(place == 64 * half + 8 * k + x, here, block)
        top_half[j] = block


    owners = span // 8
    nothing = jnp.zeros((8, 128), jnp.float32)

    def hand_over(j):
        at = pl.ds(j * owners, owners)
        remote(side_part.at[at], side_mate.at[at], out_sem, chunk_sem.at[(j + 3) // 4], lead).start()

    def send_side(j, carry):
        for lot, first, end in ((0, 0, 1), (1, 1, 5), (2, 5, CHUNKS)):
            pl.when(j == first)(
                lambda: wait_all(side_mate.at[pl.ds(first * owners, (end - first) * owners)], chunk_sem.at[lot])
            )
        at = pl.ds(j * owners, owners)
        side_part[at] += side_mate[at]
        @pl.when(rows_out)
        def _():
            columns = jnp.broadcast_to(side_part[at, 0][:, :, :1], (owners, 8, 128))
            edge_part[at, 0:1] = jnp.where((iota(0) == lane)[None], columns, 0.0).sum(axis=1, keepdims=True)
            for q in range(owners):
                n = j * owners + q
                src, dst = edge_part.at[n, pl.ds(0, 1)], edge_recv.at[chip, pl.ds(0, 1)]
                remote(src, dst, out_sem, edge_in.at[2], (2 * n + 1, me_z - 1)).start()

        for q in range(owners):
            n = j * owners + q

            @pl.when(chip != n)
            def _():
                remote(side_part.at[n], side_recv.at[chip], out_sem, side_sem, (2 * n + 1, me_z)).start()

        return carry

    def send_top(z):
        remote(top_part.at[z], top_recv.at[core * nz + me_z], out_sem, top_sem.at[core], (2 * chip + 1, z)).start()

    def pack(z, above):
        here = top_half[2 * z] + top_half[2 * z + 1]
        below = jnp.where(z > 0, top_half[jnp.maximum(2 * z - 1, 0)], 0.0)
        around = jnp.where(lane == 64, above, jnp.where(lane == 127, below, 0.0))
        turned = jnp.where(lane == 64, pltpu.roll(above, 64, 1), jnp.where(lane == 127, pltpu.roll(below, 64, 1), 0.0))
        top_part[z, 0] = jnp.where(lane < 64, here, turned)
        top_part[z, 1] = jnp.where(lane < 64, pltpu.roll(here, 64, 1), around)

    def step(j, carry):
        add(j)

        @pl.when(follows)
        def _():
            @pl.when(j == 0)
            def _():
                pl.semaphore_wait(barrier, 1 + 2 * me_z)
                signal(line_sem, lead)

            hand_over(j)

            @pl.when(j == 0)
            def _():
                for z in range(nz - 1):
                    @pl.when(me_z > z)
                    def _():
                        signal(ready_sem, (2 * chip + 1, z))
                        signal(ready_sem, (2 * chip, z))

        @pl.when(jnp.logical_and(j >= 2, j % 2 == 0))
        def _():
            z = j // 2 - 1
            pack(z, top_half[j])
            pl.when(jnp.logical_and(leads, z == 0))(lambda: pl.semaphore_wait(line_sem, 1))
            pl.when(z < me_z)(lambda: send_top(z))

        return carry

    lax.fori_loop(0, CHUNKS - 1, step, 0)

    @pl.when(leads)
    def _():
        pl.when(~rows_out)(lambda: pl.semaphore_wait(barrier, chips - 1))
        pl.when(rows_out)(lambda: pl.semaphore_wait(barrier, 2 * chips - 1))
        lax.fori_loop(0, 2, send_side, 0)

    lax.fori_loop(CHUNKS - 1, CHUNKS, step, 0)

    def send_up():
        pl.when(me_z < nz - 1)(lambda: pl.semaphore_wait(ready_sem, nz - 1 - me_z))
        for z in range(1, nz):
            pl.when(me_z < z)(lambda: send_top(z))

    up, down = 2 * chip + 3, 2 * chip - 1
    last = chip == chips - 1
    first_in, first_out = (chip == 0) & (me_z == 0), (chip == 0) & (me_z == 1)
    passes = rows_in & ~first_in
    totals = (
        (side_total, side_halo, ~last, chip > 0, (up - 1, me_z), 0, edge_in.at[0]),
        (side_total, side_halo, chip > 0, ~last, (down, me_z), 1, edge_in.at[0]),
        (side_total.at[1], side_low, ~top, me_z > 0, (me_y, me_z + 1), 2, edge_in.at[1]),
        (side_total.at[1], side_low, ~top, me_z > 0, (2 * chip, me_z + 1), 2, edge_in.at[1]),
        (side_high.at[pl.ds(0, 1)], side_high.at[pl.ds(0, 1)], passes, passes, mate, 3, edge_in.at[2]),
        (side_total, side_total, leads, follows, mate, 4, side_sem),
        (top_total.at[3], top_halo, ~last, chip > 0, (up - 1, me_z), 0, edge_in.at[3]),
        (top_total.at[0], top_halo, chip > 0, ~last, (down, me_z), 1, edge_in.at[3]),
        (top_total, top_total, leads, follows, mate, 4, top_sem.at[0]),
        (side_total.at[0], side_next, next_out, next_in, (me_y, me_z - 1), 5, edge_in.at[2]),
        (side_total.at[0], side_next, next_out | first_out, next_in | first_in, (2 * chip, me_z - 1), 5, edge_in.at[2]),
    )

    def total(k):
        src, dst, _, _, peer, send, recv = totals[k]
        return remote(src, dst, edge_out.at[send], recv, peer)

    def send_totals(*which):
        for k in which:
            pl.when(totals[k][2])(lambda: total(k).start())

    def wait_totals(*which):
        for k in which:
            pl.when(totals[k][3])(lambda: total(k).wait_recv())

    @pl.when(me_z == 0)
    def _():
        side_low[...] = nothing

    @pl.when(~rows_in)
    def _():
        side_high[...] = nothing

    @pl.when(me_y % (ny - 1) == 0)
    def _():
        side_halo[...] = jnp.zeros((2, 8, 128), jnp.float32)
        top_halo[...] = nothing

    def make_side(shift):
        beside = [side_halo[h] for h in range(2)]
        parts = [side_total[h] for h in range(2)]
        high = jnp.where(iota(0) == lane, jnp.broadcast_to(side_high[0:1], (8, 128)), 0.0).sum(axis=1, keepdims=True)
        high = jnp.where(next_in if shift else next_in | first_in, side_next[...], jnp.broadcast_to(high, (8, 128)))
        for h, maps in enumerate(side_maps(parts, beside, beside, side_low[...], high, y_factor)):
            for i in range(3):
                maps_out[2 * i + h] = pltpu.roll(maps[i], 4, 0) if shift else maps[i]

    def make_top(below, parts, above):
        for h, maps in enumerate(top_maps(below, parts, above, z_factor)):
            for i in range(3):
                maps_out[6 + 2 * i + h] = maps[i]

    @pl.when(follows)
    def _():
        pack(nz - 1, nothing)
        send_top(me_z)
        send_up()
        wait_totals(8, 6)
        make_top(top_halo[...], [top_total[0], top_total[1]], top_total[2])
        wait_totals(5, 0, 3, 4, 10)
        make_side(False)
        wait_all(cells.at[pl.ds(0, (2 * chips + 2 * nz) // tiles)], out_sem)

    @pl.when(leads)
    def _():
        lax.fori_loop(2, CHUNKS, send_side, 0)
        pack(nz - 1, nothing)
        send_up()
        side_recv[chip] = side_part[chip]
        top_recv[nz + me_z] = top_part[me_z]

        wait_all(side_recv.at[pl.ds(0, chips - 1)], side_sem)
        side_total[...] = side_recv[...].sum(axis=0)
        send_totals(9, 10, 2, 3, 1, 0, 5)

        wait_all(top_recv.at[pl.ds(0, nz - 1)], top_sem.at[1])
        top_total[2:4] = top_recv[nz : 2 * nz].sum(axis=0)
        send_totals(6)
        wait_all(top_recv.at[pl.ds(0, nz)], top_sem.at[0])
        top_total[0:2] = top_recv[0:nz].sum(axis=0)
        send_totals(7, 8)

        @pl.when(rows_in)
        def _():
            wait_all(edge_recv.at[pl.ds(0, chips), pl.ds(0, 1)], edge_in.at[2])
            side_high[0:1] = edge_recv[:, 0:1].sum(axis=0)

        send_totals(4)
        sent = 2 * (chips - 1) + 2 * (nz - 1)
        pl.when(~rows_out)(lambda: wait_all(cells.at[pl.ds(0, sent // tiles)], out_sem))
        pl.when(rows_out)(lambda: wait_all(cells.at[pl.ds(0, (sent + chips // 8) // tiles)], out_sem))
        wait_totals(7)
        make_top(top_total[1], [top_total[2], top_total[3]], top_halo[...])
        for send, (out, count) in enumerate(((~last, 3), (chip > 0, 3), (~top, 2))):
            pl.when(out)(lambda: wait_all(top_total.at[pl.ds(0, count)], edge_out.at[send]))
        wait_totals(1, 2, 9)
        make_side(True)
        pl.when(passes)(lambda: wait_all(side_high.at[pl.ds(0, 1)], edge_out.at[3]))
        wait_all(top_part.at[pl.ds(0, 3)], edge_out.at[4])
        pl.when(next_out)(lambda: wait_all(top_total.at[pl.ds(0, 2)], edge_out.at[5]))
        pl.when(first_out)(lambda: wait_all(side_next, edge_out.at[5]))


def unpack(maps, side_out, top_out):
    for i in range(3):
        side_out[i, :, 0:128] = maps[2 * i, :4]
        side_out[i, :, 128:256] = maps[2 * i + 1, :4]
        top_out[i, 0:8, :] = maps[6 + 2 * i, :, :64]
        top_out[i, 8:16, :] = maps[7 + 2 * i, :, :64]


def solution(mesh):
    ny, nz = mesh.shape["gy"], mesh.shape["gz"]
    chips = ny // 2

    def body(density):
        rows, depth, width = density.shape

        def blocks(*count):
            return pltpu.VMEM((*count, 8, 128), jnp.float32)

        vmem = pl.BlockSpec(memory_space=pltpu.VMEM)
        maps = pl.pallas_call(
            functools.partial(kernel, ny, nz, 1.0 / math.sqrt(depth * ny), 1.0 / math.sqrt(width * nz)),
            out_shape=pltpu.VMEM((12, 8, 128), jnp.float32),
            in_specs=[pl.BlockSpec(memory_space=pltpu.HBM)],
            out_specs=vmem,
            scratch_shapes=[
                pltpu.VMEM((rows, depth, width), jnp.float32),
                blocks(chips, 2),
                blocks(chips, 2),
                blocks(chips, 2),
                blocks(2),
                blocks(2),
                blocks(),
                blocks(),
                blocks(),
                blocks(chips),
                blocks(chips),
                blocks(CHUNKS),
                blocks(nz, 2),
                blocks(2 * nz, 2),
                blocks(4),
                blocks(),
                pltpu.SemaphoreType.DMA((LOADS,)),
                pltpu.SemaphoreType.DMA((3,)),
                pltpu.SemaphoreType.DMA,
                pltpu.SemaphoreType.DMA,
                pltpu.SemaphoreType.DMA((2,)),
                pltpu.SemaphoreType.DMA((6,)),
                pltpu.SemaphoreType.DMA((4,)),
                pltpu.SemaphoreType.REGULAR,
                pltpu.SemaphoreType.REGULAR,
            ],
            compiler_params=pltpu.CompilerParams(
                collective_id=0, has_side_effects=True, vmem_limit_bytes=16 * 1024 * 1024
            ),
            name="views",
        )(pltpu.with_memory_space_constraint(density, pltpu.HBM))
        side, top = pl.pallas_call(
            unpack,
            out_shape=(
                jax.ShapeDtypeStruct((3, rows // ny, width), jnp.float32),
                jax.ShapeDtypeStruct((3, depth, rows // nz), jnp.float32),
            ),
            in_specs=[vmem],
            out_specs=(vmem, vmem),
            name="unpack",
        )(pltpu.with_memory_space_constraint(maps, pltpu.VMEM))
        return side, jnp.swapaxes(top, 1, 2)

    return jax.shard_map(
        body,
        mesh=mesh,
        in_specs=(P(None, "gy", "gz"),),
        out_specs=(P(None, "gy", "gz"), P(None, "gz", "gy")),
        check_vma=False,
    )
```

```python
import functools
import math

import jax
import jax.numpy as jnp
from jax import lax
from jax.experimental import pallas as pl
from jax.experimental.pallas import tpu as pltpu
from jax.sharding import PartitionSpec as P

MESH = pl.DeviceIdType.MESH
CHUNKS = 8
LOADS = 8


def iota(axis):
    return lax.broadcasted_iota(jnp.int32, (8, 128), axis)


def stencil(here, lower_a, upper_a, lower_x, upper_x, factor):
    return (
        (upper_a - lower_a) * (0.5 * factor),
        (upper_x - lower_x) * (0.5 * factor),
        (upper_x + lower_x + upper_a + lower_a - 4.0 * here) * factor,
    )


def side_maps(parts, low_x, high_x, low_z, high_z, factor):
    row, lane = iota(0), iota(1)
    around = (low_z, *parts, high_z)
    for h, here in enumerate(parts):
        yield stencil(
            here,
            pltpu.roll(jnp.where(lane == 127, around[h], here), 1, 1),
            pltpu.roll(jnp.where(lane == 0, around[h + 2], here), 127, 1),
            pltpu.roll(jnp.where(row == 7, low_x[h], here), 1, 0),
            pltpu.roll(jnp.where(row == 0, high_x[h], here), 7, 0),
            factor,
        )


def top_maps(below, parts, above, factor):
    row = iota(0)
    around = (below, *parts, above)
    for h, here in enumerate(parts):
        yield stencil(
            here,
            pltpu.roll(jnp.where(row == 7, around[h], here), 1, 0),
            pltpu.roll(jnp.where(row == 0, around[h + 2], here), 7, 0),
            pltpu.roll(here, 1, 1),
            pltpu.roll(here, 127, 1),
            factor,
        )


def kernel(ny, nz, y_factor, z_factor, density, maps_out, cells, side_part, side_mate, side_recv, side_total, side_halo, side_low, side_high, side_next, edge_part, edge_recv,
           top_half, top_part, top_recv, top_total, top_halo, load_sem, chunk_sem, out_sem, side_sem, top_sem, edge_out,
           edge_in, line_sem, ready_sem):
    rows, depth, width = cells.shape
    span = rows // CHUNKS
    chips = ny // 2
    tiles = depth * width // 1024
    me_y, me_z = lax.axis_index("gy"), lax.axis_index("gz")
    chip, core = me_y // 2, me_y % 2
    leads, follows = core == 1, core == 0
    top = me_z == nz - 1
    rows_in, rows_out = me_z < nz // 2, (me_z > 0) & (me_z <= nz // 2)
    next_in, next_out = (me_z >= nz // 2) & ~top, me_z > nz // 2
    lead, mate = (2 * chip + 1, me_z), (2 * chip, me_z)

    def load(i):
        at = pl.ds(i * (rows // LOADS), rows // LOADS)
        return pltpu.make_async_copy(density.at[at], cells.at[at], load_sem.at[i])

    for i in range(LOADS):
        load(i).start()

    def remote(src, dst, send, recv, peer):
        return pltpu.make_async_remote_copy(
            src_ref=src, dst_ref=dst, send_sem=send, recv_sem=recv, device_id=peer, device_id_type=MESH
        )

    def signal(sem, peer):
        pl.semaphore_signal(sem, inc=1, device_id=peer, device_id_type=MESH)

    def wait_all(ref, sem):
        pltpu.make_async_copy(ref, ref, sem).wait()

    barrier = pltpu.get_barrier_semaphore()

    for z in range(1, nz):
        pl.when(me_z < z)(lambda: signal(barrier, (2 * chip, z)))

    @pl.when(leads)
    def _():
        signal(barrier, mate)
        for n in range(chips):
            pl.when(chip != n)(lambda: signal(barrier, (2 * n + 1, me_z)))

        @pl.when(rows_in)
        def _():
            for n in range(chips):
                signal(barrier, (2 * n + 1, me_z + 1))

    lane = iota(1)

    def add(j):
        pl.when(j % (CHUNKS // LOADS) == 0)(lambda: load(j // (CHUNKS // LOADS)).wait())
        block = jnp.zeros((8, 128), jnp.float32)
        place = lane - (j * span) % 64
        for k in range(span // 8):
            piece = cells[pl.ds(j * span + 8 * k, 8)]
            added = piece.sum(axis=1)
            side_part[j * (span // 8) + k, 0] = added[:, :128]
            side_part[j * (span // 8) + k, 1] = added[:, 128:]
            added = (piece[:, :, :128] + piece[:, :, 128:]).sum(axis=2, keepdims=True)
            for x in range(8):
                for half in range(2):
                    here = added[x, 8 * half : 8 * half + 8]
                    block = jnp.where(place == 64 * half + 8 * k + x, here, block)
        top_half[j] = block


    owners = span // 8
    nothing = jnp.zeros((8, 128), jnp.float32)

    def hand_over(j):
        at = pl.ds(j * owners, owners)
        remote(side_part.at[at], side_mate.at[at], out_sem, chunk_sem.at[(j + 3) // 4], lead).start()

    def send_side(j, carry):
        for lot, first, end in ((0, 0, 1), (1, 1, 5), (2, 5, CHUNKS)):
            pl.when(j == first)(
                lambda: wait_all(side_mate.at[pl.ds(first * owners, (end - first) * owners)], chunk_sem.at[lot])
            )
        at = pl.ds(j * owners, owners)
        side_part[at] += side_mate[at]
        @pl.when(rows_out)
        def _():
            columns = jnp.broadcast_to(side_part[at, 0][:, :, :1], (owners, 8, 128))
            edge_part[at, 0:1] = jnp.where((iota(0) == lane)[None], columns, 0.0).sum(axis=1, keepdims=True)
            for q in range(owners):
                n = j * owners + q
                src, dst = edge_part.at[n, pl.ds(0, 1)], edge_recv.at[chip, pl.ds(0, 1)]
                remote(src, dst, out_sem, edge_in.at[2], (2 * n + 1, me_z - 1)).start()

        for q in range(owners):
            n = j * owners + q

            @pl.when(chip != n)
            def _():
                remote(side_part.at[n], side_recv.at[chip], out_sem, side_sem, (2 * n + 1, me_z)).start()

        return carry

    def send_top(z):
        remote(top_part.at[z], top_recv.at[core * nz + me_z], out_sem, top_sem.at[core], (2 * chip + 1, z)).start()

    def pack(z, above):
        here = top_half[2 * z] + top_half[2 * z + 1]
        below = jnp.where(z > 0, top_half[jnp.maximum(2 * z - 1, 0)], 0.0)
        around = jnp.where(lane == 64, above, jnp.where(lane == 127, below, 0.0))
        turned = jnp.where(lane == 64, pltpu.roll(above, 64, 1), jnp.where(lane == 127, pltpu.roll(below, 64, 1), 0.0))
        top_part[z, 0] = jnp.where(lane < 64, here, turned)
        top_part[z, 1] = jnp.where(lane < 64, pltpu.roll(here, 64, 1), around)

    def step(j, carry):
        add(j)

        @pl.when(follows)
        def _():
            @pl.when(j == 0)
            def _():
                pl.semaphore_wait(barrier, 1 + 2 * me_z)
                signal(line_sem, lead)

            hand_over(j)

            @pl.when(j == 0)
            def _():
                for z in range(nz - 1):
                    @pl.when(me_z > z)
                    def _():
                        signal(ready_sem, (2 * chip + 1, z))
                        signal(ready_sem, (2 * chip, z))

        @pl.when(jnp.logical_and(j >= 2, j % 2 == 0))
        def _():
            z = j // 2 - 1
            pack(z, top_half[j])
            pl.when(jnp.logical_and(leads, z == 0))(lambda: pl.semaphore_wait(line_sem, 1))
            pl.when(z < me_z)(lambda: send_top(z))

        return carry

    lax.fori_loop(0, CHUNKS - 1, step, 0)

    @pl.when(leads)
    def _():
        pl.when(~rows_out)(lambda: pl.semaphore_wait(barrier, chips - 1))
        pl.when(rows_out)(lambda: pl.semaphore_wait(barrier, 2 * chips - 1))
        lax.fori_loop(0, 2, send_side, 0)

    lax.fori_loop(CHUNKS - 1, CHUNKS, step, 0)

    def send_up():
        pl.when(me_z < nz - 1)(lambda: pl.semaphore_wait(ready_sem, nz - 1 - me_z))
        for z in range(1, nz):
            pl.when(me_z < z)(lambda: send_top(z))

    up, down = ((2 * chip + 2) % ny, me_z), ((2 * chip + ny - 1) % ny, me_z)
    above, below = (me_z + 1) % nz, (me_z + nz - 1) % nz
    last = chip == chips - 1
    first_in, first_out = (chip == 0) & (me_z == 0), (chip == 0) & (me_z == 1)
    passes = rows_in & ~first_in
    totals = (
        (side_total, side_halo, ~last, chip > 0, up, 0, edge_in.at[0]),
        (side_total, side_halo, chip > 0, ~last, down, 1, edge_in.at[0]),
        (side_total.at[1], side_low, ~top, me_z > 0, (me_y, above), 2, edge_in.at[1]),
        (side_total.at[1], side_low, ~top, me_z > 0, (2 * chip, above), 2, edge_in.at[1]),
        (side_high.at[pl.ds(0, 1)], side_high.at[pl.ds(0, 1)], passes, passes, mate, 3, edge_in.at[2]),
        (side_total, side_total, leads, follows, mate, 4, side_sem),
        (top_total.at[3], top_halo, ~last, chip > 0, up, 0, edge_in.at[3]),
        (top_total.at[0], top_halo, chip > 0, ~last, down, 1, edge_in.at[3]),
        (top_total, top_total, leads, follows, mate, 4, top_sem.at[0]),
        (side_total.at[0], side_next, next_out, next_in, (me_y, below), 5, edge_in.at[2]),
        (side_total.at[0], side_next, next_out | first_out, next_in | first_in, (2 * chip, below), 5, edge_in.at[2]),
    )

    def total(k):
        src, dst, _, _, peer, send, recv = totals[k]
        return remote(src, dst, edge_out.at[send], recv, peer)

    def send_totals(*which):
        for k in which:
            pl.when(totals[k][2])(lambda: total(k).start())

    def wait_totals(*which):
        for k in which:
            pl.when(totals[k][3])(lambda: total(k).wait_recv())

    @pl.when(me_z == 0)
    def _():
        side_low[...] = nothing

    @pl.when(~rows_in)
    def _():
        side_high[...] = nothing

    @pl.when(me_y % (ny - 1) == 0)
    def _():
        side_halo[...] = jnp.zeros((2, 8, 128), jnp.float32)
        top_halo[...] = nothing

    def make_side(shift):
        beside = [side_halo[h] for h in range(2)]
        parts = [side_total[h] for h in range(2)]
        high = jnp.where(iota(0) == lane, jnp.broadcast_to(side_high[0:1], (8, 128)), 0.0).sum(axis=1, keepdims=True)
        high = jnp.where(next_in if shift else next_in | first_in, side_next[...], jnp.broadcast_to(high, (8, 128)))
        for h, maps in enumerate(side_maps(parts, beside, beside, side_low[...], high, y_factor)):
            for i in range(3):
                maps_out[2 * i + h] = pltpu.roll(maps[i], 4, 0) if shift else maps[i]

    def make_top(below, parts, above):
        for h, maps in enumerate(top_maps(below, parts, above, z_factor)):
            for i in range(3):
                maps_out[6 + 2 * i + h] = maps[i]

    @pl.when(follows)
    def _():
        pack(nz - 1, nothing)
        send_top(me_z)
        send_up()
        wait_totals(8, 6)
        make_top(top_halo[...], [top_total[0], top_total[1]], top_total[2])
        wait_totals(5, 0, 3, 4, 10)
        make_side(False)
        wait_all(cells.at[pl.ds(0, (2 * chips + 2 * nz) // tiles)], out_sem)

    @pl.when(leads)
    def _():
        lax.fori_loop(2, CHUNKS, send_side, 0)
        pack(nz - 1, nothing)
        send_up()
        side_recv[chip] = side_part[chip]
        top_recv[nz + me_z] = top_part[me_z]

        wait_all(side_recv.at[pl.ds(0, chips - 1)], side_sem)
        side_total[...] = side_recv[...].sum(axis=0)
        send_totals(9, 10, 2, 3, 1, 0, 5)

        wait_all(top_recv.at[pl.ds(0, nz - 1)], top_sem.at[1])
        top_total[2:4] = top_recv[nz : 2 * nz].sum(axis=0)
        send_totals(6)
        wait_all(top_recv.at[pl.ds(0, nz)], top_sem.at[0])
        top_total[0:2] = top_recv[0:nz].sum(axis=0)
        send_totals(7, 8)

        wait_totals(7)
        make_top(top_total[1], [top_total[2], top_total[3]], top_halo[...])

        @pl.when(rows_in)
        def _():
            wait_all(edge_recv.at[pl.ds(0, chips), pl.ds(0, 1)], edge_in.at[2])
            side_high[0:1] = edge_recv[:, 0:1].sum(axis=0)

        send_totals(4)
        sent = 2 * (chips - 1) + 2 * (nz - 1)
        pl.when(~rows_out)(lambda: wait_all(cells.at[pl.ds(0, sent // tiles)], out_sem))
        pl.when(rows_out)(lambda: wait_all(cells.at[pl.ds(0, (sent + chips // 8) // tiles)], out_sem))
        for send, (out, count) in enumerate(((~last, 3), (chip > 0, 3), (~top, 2))):
            pl.when(out)(lambda: wait_all(top_total.at[pl.ds(0, count)], edge_out.at[send]))
        wait_totals(1, 2, 9)
        make_side(True)
        pl.when(passes)(lambda: wait_all(side_high.at[pl.ds(0, 1)], edge_out.at[3]))
        wait_all(top_part.at[pl.ds(0, 3)], edge_out.at[4])
        pl.when(next_out)(lambda: wait_all(top_total.at[pl.ds(0, 2)], edge_out.at[5]))
        pl.when(first_out)(lambda: wait_all(side_next, edge_out.at[5]))


def unpack(maps, side_out, top_out):
    for i in range(3):
        side_out[i, :, 0:128] = maps[2 * i, :4]
        side_out[i, :, 128:256] = maps[2 * i + 1, :4]
        top_out[i, 0:8, :] = maps[6 + 2 * i, :, :64]
        top_out[i, 8:16, :] = maps[7 + 2 * i, :, :64]


def solution(mesh):
    ny, nz = mesh.shape["gy"], mesh.shape["gz"]
    chips = ny // 2

    def body(density):
        rows, depth, width = density.shape

        def blocks(*count):
            return pltpu.VMEM((*count, 8, 128), jnp.float32)

        vmem = pl.BlockSpec(memory_space=pltpu.VMEM)
        maps = pl.pallas_call(
            functools.partial(kernel, ny, nz, 1.0 / math.sqrt(depth * ny), 1.0 / math.sqrt(width * nz)),
            out_shape=pltpu.VMEM((12, 8, 128), jnp.float32),
            in_specs=[pl.BlockSpec(memory_space=pltpu.HBM)],
            out_specs=vmem,
            scratch_shapes=[
                pltpu.VMEM((rows, depth, width), jnp.float32),
                blocks(chips, 2),
                blocks(chips, 2),
                blocks(chips, 2),
                blocks(2),
                blocks(2),
                blocks(),
                blocks(),
                blocks(),
                blocks(chips),
                blocks(chips),
                blocks(CHUNKS),
                blocks(nz, 2),
                blocks(2 * nz, 2),
                blocks(4),
                blocks(),
                pltpu.SemaphoreType.DMA((LOADS,)),
                pltpu.SemaphoreType.DMA((3,)),
                pltpu.SemaphoreType.DMA,
                pltpu.SemaphoreType.DMA,
                pltpu.SemaphoreType.DMA((2,)),
                pltpu.SemaphoreType.DMA((6,)),
                pltpu.SemaphoreType.DMA((4,)),
                pltpu.SemaphoreType.REGULAR,
                pltpu.SemaphoreType.REGULAR,
            ],
            compiler_params=pltpu.CompilerParams(
                collective_id=0, has_side_effects=True, vmem_limit_bytes=16 * 1024 * 1024
            ),
            name="views",
        )(pltpu.with_memory_space_constraint(density, pltpu.HBM))
        side, top = pl.pallas_call(
            unpack,
            out_shape=(
                jax.ShapeDtypeStruct((3, rows // ny, width), jnp.float32),
                jax.ShapeDtypeStruct((3, depth, rows // nz), jnp.float32),
            ),
            in_specs=[vmem],
            out_specs=(vmem, vmem),
            name="unpack",
        )(pltpu.with_memory_space_constraint(maps, pltpu.VMEM))
        return side, jnp.swapaxes(top, 1, 2)

    return jax.shard_map(
        body,
        mesh=mesh,
        in_specs=(P(None, "gy", "gz"),),
        out_specs=(P(None, "gy", "gz"), P(None, "gz", "gy")),
        check_vma=False,
    )
```

```python
import functools
import math

import jax
import jax.numpy as jnp
from jax import lax
from jax.experimental import pallas as pl
from jax.experimental.pallas import tpu as pltpu
from jax.sharding import PartitionSpec as P

MESH = pl.DeviceIdType.MESH
CHUNKS = 8
LOADS = ((0, 1), (1, 2), (3, 2), (5, 3))


def iota(axis):
    return lax.broadcasted_iota(jnp.int32, (8, 128), axis)


def stencil(here, lower_a, upper_a, lower_x, upper_x, factor):
    return (
        (upper_a - lower_a) * (0.5 * factor),
        (upper_x - lower_x) * (0.5 * factor),
        (upper_x + lower_x + upper_a + lower_a - 4.0 * here) * factor,
    )


def side_maps(parts, low_x, high_x, low_z, high_z, factor):
    row, lane = iota(0), iota(1)
    around = (low_z, *parts, high_z)
    for h, here in enumerate(parts):
        yield stencil(
            here,
            pltpu.roll(jnp.where(lane == 127, around[h], here), 1, 1),
            pltpu.roll(jnp.where(lane == 0, around[h + 2], here), 127, 1),
            pltpu.roll(jnp.where(row == 7, low_x[h], here), 1, 0),
            pltpu.roll(jnp.where(row == 0, high_x[h], here), 7, 0),
            factor,
        )


def top_maps(below, parts, above, factor):
    row = iota(0)
    around = (below, *parts, above)
    for h, here in enumerate(parts):
        yield stencil(
            here,
            pltpu.roll(jnp.where(row == 7, around[h], here), 1, 0),
            pltpu.roll(jnp.where(row == 0, around[h + 2], here), 7, 0),
            pltpu.roll(here, 1, 1),
            pltpu.roll(here, 127, 1),
            factor,
        )


def kernel(ny, nz, y_factor, z_factor, density, maps_out, cells, side_part, side_mate, side_recv, side_total, side_halo, side_low, side_high, side_next, edge_part, edge_recv,
           top_half, top_part, top_recv, top_total, top_halo, load_sem, chunk_sem, out_sem, side_sem, top_sem, edge_out,
           edge_in, line_sem, ready_sem):
    rows, depth, width = cells.shape
    span = rows // CHUNKS
    chips = ny // 2
    tiles = depth * width // 1024
    me_y, me_z = lax.axis_index("gy"), lax.axis_index("gz")
    chip, core = me_y // 2, me_y % 2
    leads, follows = core == 1, core == 0
    top = me_z == nz - 1
    rows_in, rows_out = me_z < nz // 2, (me_z > 0) & (me_z <= nz // 2)
    next_in, next_out = (me_z >= nz // 2) & ~top, me_z > nz // 2
    lead, mate = (2 * chip + 1, me_z), (2 * chip, me_z)

    def load(i):
        first, count = LOADS[i]
        at = pl.ds(first * span, count * span)
        return pltpu.make_async_copy(density.at[at], cells.at[at], load_sem.at[i])

    for i in range(len(LOADS)):
        load(i).start()

    def remote(src, dst, send, recv, peer):
        return pltpu.make_async_remote_copy(
            src_ref=src, dst_ref=dst, send_sem=send, recv_sem=recv, device_id=peer, device_id_type=MESH
        )

    def signal(sem, peer):
        pl.semaphore_signal(sem, inc=1, device_id=peer, device_id_type=MESH)

    def wait_all(ref, sem):
        pltpu.make_async_copy(ref, ref, sem).wait()

    barrier = pltpu.get_barrier_semaphore()

    for z in range(1, nz):
        pl.when(me_z < z)(lambda: signal(barrier, (2 * chip, z)))

    @pl.when(leads)
    def _():
        signal(barrier, mate)
        for n in range(chips):
            pl.when(chip != n)(lambda: signal(barrier, (2 * n + 1, me_z)))

        @pl.when(rows_in)
        def _():
            for n in range(chips):
                signal(barrier, (2 * n + 1, me_z + 1))

    lane = iota(1)

    def add(j):
        for i, (first, _) in enumerate(LOADS):
            pl.when(j == first)(lambda: load(i).wait())
        block = jnp.zeros((8, 128), jnp.float32)
        place = lane - (j * span) % 64
        for k in range(span // 8):
            piece = cells[pl.ds(j * span + 8 * k, 8)]
            added = piece.sum(axis=1)
            side_part[j * (span // 8) + k, 0] = added[:, :128]
            side_part[j * (span // 8) + k, 1] = added[:, 128:]
            added = (piece[:, :, :128] + piece[:, :, 128:]).sum(axis=2, keepdims=True)
            for x in range(8):
                for half in range(2):
                    here = added[x, 8 * half : 8 * half + 8]
                    block = jnp.where(place == 64 * half + 8 * k + x, here, block)
        top_half[j] = block


    owners = span // 8
    nothing = jnp.zeros((8, 128), jnp.float32)

    def hand_over(j):
        at = pl.ds(j * owners, owners)
        remote(side_part.at[at], side_mate.at[at], out_sem, chunk_sem.at[(j + 3) // 4], lead).start()

    def send_side(j, carry):
        for lot, first, end in ((0, 0, 1), (1, 1, 5), (2, 5, CHUNKS)):
            pl.when(j == first)(
                lambda: wait_all(side_mate.at[pl.ds(first * owners, (end - first) * owners)], chunk_sem.at[lot])
            )
        at = pl.ds(j * owners, owners)
        side_part[at] += side_mate[at]
        @pl.when(rows_out)
        def _():
            columns = jnp.broadcast_to(side_part[at, 0][:, :, :1], (owners, 8, 128))
            edge_part[at, 0:1] = jnp.where((iota(0) == lane)[None], columns, 0.0).sum(axis=1, keepdims=True)
            for q in range(owners):
                n = j * owners + q
                src, dst = edge_part.at[n, pl.ds(0, 1)], edge_recv.at[chip, pl.ds(0, 1)]
                remote(src, dst, out_sem, edge_in.at[2], (2 * n + 1, me_z - 1)).start()

        for q in range(owners):
            n = j * owners + q

            @pl.when(chip != n)
            def _():
                remote(side_part.at[n], side_recv.at[chip], out_sem, side_sem, (2 * n + 1, me_z)).start()

        return carry

    def send_top(z):
        remote(top_part.at[z], top_recv.at[core * nz + me_z], out_sem, top_sem.at[core], (2 * chip + 1, z)).start()

    def pack(z, above):
        here = top_half[2 * z] + top_half[2 * z + 1]
        below = jnp.where(z > 0, top_half[jnp.maximum(2 * z - 1, 0)], 0.0)
        around = jnp.where(lane == 64, above, jnp.where(lane == 127, below, 0.0))
        turned = jnp.where(lane == 64, pltpu.roll(above, 64, 1), jnp.where(lane == 127, pltpu.roll(below, 64, 1), 0.0))
        top_part[z, 0] = jnp.where(lane < 64, here, turned)
        top_part[z, 1] = jnp.where(lane < 64, pltpu.roll(here, 64, 1), around)

    def step(j, carry):
        add(j)

        @pl.when(follows)
        def _():
            @pl.when(j == 0)
            def _():
                pl.semaphore_wait(barrier, 1 + 2 * me_z)
                signal(line_sem, lead)

            hand_over(j)

            @pl.when(j == 0)
            def _():
                for z in range(nz - 1):
                    @pl.when(me_z > z)
                    def _():
                        signal(ready_sem, (2 * chip + 1, z))
                        signal(ready_sem, (2 * chip, z))

        @pl.when(jnp.logical_and(j >= 2, j % 2 == 0))
        def _():
            z = j // 2 - 1
            pack(z, top_half[j])
            pl.when(jnp.logical_and(leads, z == 0))(lambda: pl.semaphore_wait(line_sem, 1))
            pl.when(z < me_z)(lambda: send_top(z))

        return carry

    lax.fori_loop(0, CHUNKS - 1, step, 0)

    @pl.when(leads)
    def _():
        pl.when(~rows_out)(lambda: pl.semaphore_wait(barrier, chips - 1))
        pl.when(rows_out)(lambda: pl.semaphore_wait(barrier, 2 * chips - 1))
        lax.fori_loop(0, 4, send_side, 0)

    lax.fori_loop(CHUNKS - 1, CHUNKS, step, 0)

    def send_up():
        pl.when(me_z < nz - 1)(lambda: pl.semaphore_wait(ready_sem, nz - 1 - me_z))
        for z in range(1, nz):
            pl.when(me_z < z)(lambda: send_top(z))

    up, down = ((2 * chip + 2) % ny, me_z), ((2 * chip + ny - 1) % ny, me_z)
    above, below = (me_z + 1) % nz, (me_z + nz - 1) % nz
    last = chip == chips - 1
    first_in, first_out = (chip == 0) & (me_z == 0), (chip == 0) & (me_z == 1)
    passes = rows_in & ~first_in
    totals = (
        (side_total, side_halo, ~last, chip > 0, up, 0, edge_in.at[0]),
        (side_total, side_halo, chip > 0, ~last, down, 1, edge_in.at[0]),
        (side_total.at[1], side_low, ~top, me_z > 0, (me_y, above), 2, edge_in.at[1]),
        (side_total.at[1], side_low, ~top, me_z > 0, (2 * chip, above), 2, edge_in.at[1]),
        (side_high.at[pl.ds(0, 1)], side_high.at[pl.ds(0, 1)], passes, passes, mate, 3, edge_in.at[2]),
        (side_total, side_total, leads, follows, mate, 4, side_sem),
        (top_total.at[3], top_halo, ~last, chip > 0, up, 0, edge_in.at[3]),
        (top_total.at[0], top_halo, chip > 0, ~last, down, 1, edge_in.at[3]),
        (top_total, top_total, leads, follows, mate, 4, top_sem.at[0]),
        (side_total.at[0], side_next, next_out, next_in, (me_y, below), 5, edge_in.at[2]),
        (side_total.at[0], side_next, next_out | first_out, next_in | first_in, (2 * chip, below), 5, edge_in.at[2]),
    )

    def total(k):
        src, dst, _, _, peer, send, recv = totals[k]
        return remote(src, dst, edge_out.at[send], recv, peer)

    def send_totals(*which):
        for k in which:
            pl.when(totals[k][2])(lambda: total(k).start())

    def wait_totals(*which):
        for k in which:
            pl.when(totals[k][3])(lambda: total(k).wait_recv())

    @pl.when(me_z == 0)
    def _():
        side_low[...] = nothing

    @pl.when(~rows_in)
    def _():
        side_high[...] = nothing

    @pl.when(me_y % (ny - 1) == 0)
    def _():
        side_halo[...] = jnp.zeros((2, 8, 128), jnp.float32)
        top_halo[...] = nothing

    def make_side(shift):
        beside = [side_halo[h] for h in range(2)]
        parts = [side_total[h] for h in range(2)]
        high = jnp.where(iota(0) == lane, jnp.broadcast_to(side_high[0:1], (8, 128)), 0.0).sum(axis=1, keepdims=True)
        high = jnp.where(next_in if shift else next_in | first_in, side_next[...], jnp.broadcast_to(high, (8, 128)))
        for h, maps in enumerate(side_maps(parts, beside, beside, side_low[...], high, y_factor)):
            for i in range(3):
                maps_out[2 * i + h] = pltpu.roll(maps[i], 4, 0) if shift else maps[i]

    def make_top(below, parts, above):
        for h, maps in enumerate(top_maps(below, parts, above, z_factor)):
            for i in range(3):
                maps_out[6 + 2 * i + h] = maps[i]

    @pl.when(follows)
    def _():
        pack(nz - 1, nothing)
        send_top(me_z)
        send_up()
        wait_totals(8, 6)
        make_top(top_halo[...], [top_total[0], top_total[1]], top_total[2])
        wait_totals(5, 0, 3, 4, 10)
        make_side(False)
        wait_all(cells.at[pl.ds(0, (2 * chips + 2 * nz) // tiles)], out_sem)

    @pl.when(leads)
    def _():
        lax.fori_loop(4, CHUNKS, send_side, 0)
        pack(nz - 1, nothing)
        send_up()
        side_recv[chip] = side_part[chip]
        top_recv[nz + me_z] = top_part[me_z]

        wait_all(side_recv.at[pl.ds(0, chips - 1)], side_sem)
        side_total[...] = side_recv[...].sum(axis=0)
        send_totals(9, 10, 2, 3, 1, 0, 5)

        wait_all(top_recv.at[pl.ds(0, nz - 1)], top_sem.at[1])
        top_total[2:4] = top_recv[nz : 2 * nz].sum(axis=0)
        send_totals(6)
        wait_all(top_recv.at[pl.ds(0, nz)], top_sem.at[0])
        top_total[0:2] = top_recv[0:nz].sum(axis=0)
        send_totals(7, 8)

        wait_totals(7)
        make_top(top_total[1], [top_total[2], top_total[3]], top_halo[...])

        @pl.when(rows_in)
        def _():
            wait_all(edge_recv.at[pl.ds(0, chips), pl.ds(0, 1)], edge_in.at[2])
            side_high[0:1] = edge_recv[:, 0:1].sum(axis=0)

        send_totals(4)
        sent = 2 * (chips - 1) + 2 * (nz - 1)
        pl.when(~rows_out)(lambda: wait_all(cells.at[pl.ds(0, sent // tiles)], out_sem))
        pl.when(rows_out)(lambda: wait_all(cells.at[pl.ds(0, (sent + chips // 8) // tiles)], out_sem))
        for send, (out, count) in enumerate(((~last, 3), (chip > 0, 3), (~top, 2))):
            pl.when(out)(lambda: wait_all(top_total.at[pl.ds(0, count)], edge_out.at[send]))
        wait_totals(1, 2, 9)
        make_side(True)
        pl.when(passes)(lambda: wait_all(side_high.at[pl.ds(0, 1)], edge_out.at[3]))
        wait_all(top_part.at[pl.ds(0, 3)], edge_out.at[4])
        pl.when(next_out)(lambda: wait_all(top_total.at[pl.ds(0, 2)], edge_out.at[5]))
        pl.when(first_out)(lambda: wait_all(side_next, edge_out.at[5]))


def unpack(maps, side_out, top_out):
    for i in range(3):
        side_out[i, :, 0:128] = maps[2 * i, :4]
        side_out[i, :, 128:256] = maps[2 * i + 1, :4]
        top_out[i, 0:8, :] = maps[6 + 2 * i, :, :64]
        top_out[i, 8:16, :] = maps[7 + 2 * i, :, :64]


def solution(mesh):
    ny, nz = mesh.shape["gy"], mesh.shape["gz"]
    chips = ny // 2

    def body(density):
        rows, depth, width = density.shape

        def blocks(*count):
            return pltpu.VMEM((*count, 8, 128), jnp.float32)

        vmem = pl.BlockSpec(memory_space=pltpu.VMEM)
        maps = pl.pallas_call(
            functools.partial(kernel, ny, nz, 1.0 / math.sqrt(depth * ny), 1.0 / math.sqrt(width * nz)),
            out_shape=pltpu.VMEM((12, 8, 128), jnp.float32),
            in_specs=[pl.BlockSpec(memory_space=pltpu.HBM)],
            out_specs=vmem,
            scratch_shapes=[
                pltpu.VMEM((rows, depth, width), jnp.float32),
                blocks(chips, 2),
                blocks(chips, 2),
                blocks(chips, 2),
                blocks(2),
                blocks(2),
                blocks(),
                blocks(),
                blocks(),
                blocks(chips),
                blocks(chips),
                blocks(CHUNKS),
                blocks(nz, 2),
                blocks(2 * nz, 2),
                blocks(4),
                blocks(),
                pltpu.SemaphoreType.DMA((len(LOADS),)),
                pltpu.SemaphoreType.DMA((3,)),
                pltpu.SemaphoreType.DMA,
                pltpu.SemaphoreType.DMA,
                pltpu.SemaphoreType.DMA((2,)),
                pltpu.SemaphoreType.DMA((6,)),
                pltpu.SemaphoreType.DMA((4,)),
                pltpu.SemaphoreType.REGULAR,
                pltpu.SemaphoreType.REGULAR,
            ],
            compiler_params=pltpu.CompilerParams(
                collective_id=0, has_side_effects=True, vmem_limit_bytes=16 * 1024 * 1024
            ),
            name="views",
        )(pltpu.with_memory_space_constraint(density, pltpu.HBM))
        side, top = pl.pallas_call(
            unpack,
            out_shape=(
                jax.ShapeDtypeStruct((3, rows // ny, width), jnp.float32),
                jax.ShapeDtypeStruct((3, depth, rows // nz), jnp.float32),
            ),
            in_specs=[vmem],
            out_specs=(vmem, vmem),
            name="unpack",
        )(pltpu.with_memory_space_constraint(maps, pltpu.VMEM))
        return side, jnp.swapaxes(top, 1, 2)

    return jax.shard_map(
        body,
        mesh=mesh,
        in_specs=(P(None, "gy", "gz"),),
        out_specs=(P(None, "gy", "gz"), P(None, "gz", "gy")),
        check_vma=False,
    )
```

```python
import functools
import math

import jax
import jax.numpy as jnp
from jax import lax
from jax.experimental import pallas as pl
from jax.experimental.pallas import tpu as pltpu
from jax.sharding import PartitionSpec as P

MESH = pl.DeviceIdType.MESH
CHUNKS = 8
LOADS = ((0, 1), (1, 2), (3, 2), (5, 3))


def iota(axis):
    return lax.broadcasted_iota(jnp.int32, (8, 128), axis)


def stencil(here, lower_a, upper_a, lower_x, upper_x, factor):
    return (
        (upper_a - lower_a) * (0.5 * factor),
        (upper_x - lower_x) * (0.5 * factor),
        (upper_x + lower_x + upper_a + lower_a - 4.0 * here) * factor,
    )


def side_maps(parts, low_x, high_x, low_z, high_z, factor):
    row, lane = iota(0), iota(1)
    around = (low_z, *parts, high_z)
    for h, here in enumerate(parts):
        yield stencil(
            here,
            pltpu.roll(jnp.where(lane == 127, around[h], here), 1, 1),
            pltpu.roll(jnp.where(lane == 0, around[h + 2], here), 127, 1),
            pltpu.roll(jnp.where(row == 7, low_x[h], here), 1, 0),
            pltpu.roll(jnp.where(row == 0, high_x[h], here), 7, 0),
            factor,
        )


def top_maps(below, parts, above, factor):
    row = iota(0)
    around = (below, *parts, above)
    for h, here in enumerate(parts):
        yield stencil(
            here,
            pltpu.roll(jnp.where(row == 7, around[h], here), 1, 0),
            pltpu.roll(jnp.where(row == 0, around[h + 2], here), 7, 0),
            pltpu.roll(here, 1, 1),
            pltpu.roll(here, 127, 1),
            factor,
        )


def kernel(ny, nz, y_factor, z_factor, density, maps_out, cells, side_part, side_mate, side_recv, side_total, side_halo, side_low, side_high, side_next, edge_part, edge_recv,
           top_half, top_part, top_recv, top_total, top_halo, load_sem, chunk_sem, out_sem, side_sem, top_sem, edge_out,
           edge_in, line_sem, ready_sem):
    rows, depth, width = cells.shape
    span = rows // CHUNKS
    chips = ny // 2
    tiles = depth * width // 1024
    me_y, me_z = lax.axis_index("gy"), lax.axis_index("gz")
    chip, core = me_y // 2, me_y % 2
    leads, follows = core == 1, core == 0
    top = me_z == nz - 1
    rows_in, rows_out = me_z < nz // 2, (me_z > 0) & (me_z <= nz // 2)
    next_in, next_out = (me_z >= nz // 2) & ~top, me_z > nz // 2
    lead, mate = (2 * chip + 1, me_z), (2 * chip, me_z)

    def load(i):
        first, count = LOADS[i]
        at = pl.ds(first * span, count * span)
        return pltpu.make_async_copy(density.at[at], cells.at[at], load_sem.at[i])

    for i in range(len(LOADS)):
        load(i).start()

    def remote(src, dst, send, recv, peer):
        return pltpu.make_async_remote_copy(
            src_ref=src, dst_ref=dst, send_sem=send, recv_sem=recv, device_id=peer, device_id_type=MESH
        )

    def signal(sem, peer):
        pl.semaphore_signal(sem, inc=1, device_id=peer, device_id_type=MESH)

    def wait_all(ref, sem):
        pltpu.make_async_copy(ref, ref, sem).wait()

    barrier = pltpu.get_barrier_semaphore()

    for z in range(1, nz):
        pl.when(me_z < z)(lambda: signal(barrier, (2 * chip, z)))

    @pl.when(leads)
    def _():
        signal(barrier, mate)
        for n in range(chips):
            pl.when(chip != n)(lambda: signal(barrier, (2 * n + 1, me_z)))

        @pl.when(rows_in)
        def _():
            for n in range(chips):
                signal(barrier, (2 * n + 1, me_z + 1))

    lane = iota(1)

    def add(j):
        for i, (first, _) in enumerate(LOADS):
            pl.when(j == first)(lambda: load(i).wait())
        block = jnp.zeros((8, 128), jnp.float32)
        place = lane - (j * span) % 64
        for k in range(span // 8):
            piece = cells[pl.ds(j * span + 8 * k, 8)]
            added = piece.sum(axis=1)
            side_part[j * (span // 8) + k, 0] = added[:, :128]
            side_part[j * (span // 8) + k, 1] = added[:, 128:]
            added = (piece[:, :, :128] + piece[:, :, 128:]).sum(axis=2, keepdims=True)
            for x in range(8):
                for half in range(2):
                    here = added[x, 8 * half : 8 * half + 8]
                    block = jnp.where(place == 64 * half + 8 * k + x, here, block)
        top_half[j] = block


    owners = span // 8
    nothing = jnp.zeros((8, 128), jnp.float32)

    def hand_over(j):
        at = pl.ds(j * owners, owners)
        remote(side_part.at[at], side_mate.at[at], out_sem, chunk_sem.at[(j + 3) // 4], lead).start()

    def send_side(j, carry):
        for lot, first, end in ((0, 0, 1), (1, 1, 5), (2, 5, CHUNKS)):
            pl.when(j == first)(
                lambda: wait_all(side_mate.at[pl.ds(first * owners, (end - first) * owners)], chunk_sem.at[lot])
            )
        at = pl.ds(j * owners, owners)
        side_part[at] += side_mate[at]
        @pl.when(rows_out)
        def _():
            columns = jnp.broadcast_to(side_part[at, 0][:, :, :1], (owners, 8, 128))
            edge_part[at, 0:1] = jnp.where((iota(0) == lane)[None], columns, 0.0).sum(axis=1, keepdims=True)
            for q in range(owners):
                n = j * owners + q
                src, dst = edge_part.at[n, pl.ds(0, 1)], edge_recv.at[chip, pl.ds(0, 1)]
                remote(src, dst, out_sem, edge_in.at[2], (2 * n + 1, me_z - 1)).start()

        for q in range(owners):
            n = j * owners + q

            @pl.when(chip != n)
            def _():
                remote(side_part.at[n], side_recv.at[chip], out_sem, side_sem, (2 * n + 1, me_z)).start()

        return carry

    def send_top(z):
        remote(top_part.at[z], top_recv.at[core * nz + me_z], out_sem, top_sem.at[core], (2 * chip + 1, z)).start()

    def pack(z, above):
        here = top_half[2 * z] + top_half[2 * z + 1]
        below = jnp.where(z > 0, top_half[jnp.maximum(2 * z - 1, 0)], 0.0)
        around = jnp.where(lane == 64, above, jnp.where(lane == 127, below, 0.0))
        turned = jnp.where(lane == 64, pltpu.roll(above, 64, 1), jnp.where(lane == 127, pltpu.roll(below, 64, 1), 0.0))
        top_part[z, 0] = jnp.where(lane < 64, here, turned)
        top_part[z, 1] = jnp.where(lane < 64, pltpu.roll(here, 64, 1), around)

    def step(j, carry):
        add(j)

        @pl.when(follows)
        def _():
            @pl.when(j == 0)
            def _():
                pl.semaphore_wait(barrier, 1 + 2 * me_z)
                signal(line_sem, lead)

            hand_over(j)

            @pl.when(j == 0)
            def _():
                for z in range(nz - 1):
                    @pl.when(me_z > z)
                    def _():
                        signal(ready_sem, (2 * chip + 1, z))
                        signal(ready_sem, (2 * chip, z))

        @pl.when(jnp.logical_and(j >= 2, j % 2 == 0))
        def _():
            z = j // 2 - 1
            pack(z, top_half[j])
            pl.when(jnp.logical_and(leads, z == 0))(lambda: pl.semaphore_wait(line_sem, 1))
            pl.when(z < me_z)(lambda: send_top(z))

        return carry

    lax.fori_loop(0, CHUNKS - 1, step, 0)

    @pl.when(leads)
    def _():
        pl.when(~rows_out)(lambda: pl.semaphore_wait(barrier, chips - 1))
        pl.when(rows_out)(lambda: pl.semaphore_wait(barrier, 2 * chips - 1))
        lax.fori_loop(0, 4, send_side, 0)

    lax.fori_loop(CHUNKS - 1, CHUNKS, step, 0)

    def send_up():
        pl.when(me_z < nz - 1)(lambda: pl.semaphore_wait(ready_sem, nz - 1 - me_z))
        for z in range(1, nz):
            pl.when(me_z < z)(lambda: send_top(z))

    up, down = ((2 * chip + 2) % ny, me_z), ((2 * chip + ny - 1) % ny, me_z)
    above, below = (me_z + 1) % nz, (me_z + nz - 1) % nz
    last = chip == chips - 1
    first_in, first_out = (chip == 0) & (me_z == 0), (chip == 0) & (me_z == 1)
    passes = rows_in & ~first_in
    totals = (
        (side_total, side_halo, ~last, chip > 0, up, 0, edge_in.at[0]),
        (side_total, side_halo, chip > 0, ~last, down, 1, edge_in.at[0]),
        (side_total.at[1], side_low, ~top, me_z > 0, (me_y, above), 2, edge_in.at[1]),
        (side_total.at[1], side_low, ~top, me_z > 0, (2 * chip, above), 2, edge_in.at[1]),
        (side_high.at[pl.ds(0, 1)], side_high.at[pl.ds(0, 1)], passes, passes, mate, 3, edge_in.at[2]),
        (side_total, side_total, leads, follows, mate, 4, side_sem),
        (top_total.at[3], top_halo, ~last, chip > 0, up, 0, edge_in.at[3]),
        (top_total.at[0], top_halo, chip > 0, ~last, down, 1, edge_in.at[3]),
        (top_total, top_total, leads, follows, mate, 4, top_sem.at[0]),
        (side_total.at[0], side_next, next_out, next_in, (me_y, below), 5, edge_in.at[2]),
        (side_total.at[0], side_next, next_out | first_out, next_in | first_in, (2 * chip, below), 5, edge_in.at[2]),
    )

    def total(k):
        src, dst, _, _, peer, send, recv = totals[k]
        return remote(src, dst, edge_out.at[send], recv, peer)

    def send_totals(*which):
        for k in which:
            pl.when(totals[k][2])(lambda: total(k).start())

    def wait_totals(*which):
        for k in which:
            pl.when(totals[k][3])(lambda: total(k).wait_recv())

    @pl.when(me_z == 0)
    def _():
        side_low[...] = nothing

    @pl.when(~rows_in)
    def _():
        side_high[...] = nothing

    @pl.when(me_y % (ny - 1) == 0)
    def _():
        side_halo[...] = jnp.zeros((2, 8, 128), jnp.float32)
        top_halo[...] = nothing

    def make_side(shift):
        beside = [side_halo[h] for h in range(2)]
        parts = [side_total[h] for h in range(2)]
        high = jnp.where(iota(0) == lane, jnp.broadcast_to(side_high[0:1], (8, 128)), 0.0).sum(axis=1, keepdims=True)
        high = jnp.where(next_in if shift else next_in | first_in, side_next[...], jnp.broadcast_to(high, (8, 128)))
        for h, maps in enumerate(side_maps(parts, beside, beside, side_low[...], high, y_factor)):
            for i in range(3):
                maps_out[2 * i + h] = pltpu.roll(maps[i], 4, 0) if shift else maps[i]

    def make_top(below, parts, above):
        for h, maps in enumerate(top_maps(below, parts, above, z_factor)):
            for i in range(3):
                maps_out[6 + 2 * i + h] = maps[i]

    @pl.when(follows)
    def _():
        pack(nz - 1, nothing)
        send_top(me_z)
        send_up()
        wait_totals(8, 6)
        make_top(top_halo[...], [top_total[0], top_total[1]], top_total[2])
        wait_totals(5, 0, 3, 4, 10)
        make_side(False)
        wait_all(cells.at[pl.ds(0, (2 * chips + 2 * nz) // tiles)], out_sem)

    @pl.when(leads)
    def _():
        lax.fori_loop(4, CHUNKS, send_side, 0)
        pack(nz - 1, nothing)
        send_up()
        side_recv[chip] = side_part[chip]
        top_recv[nz + me_z] = top_part[me_z]

        wait_all(side_recv.at[pl.ds(0, chips - 1)], side_sem)
        side_total[...] = side_recv[...].sum(axis=0)
        send_totals(0, 2, 3, 10, 9, 5, 1)

        wait_all(top_recv.at[pl.ds(0, nz - 1)], top_sem.at[1])
        top_total[2:4] = top_recv[nz : 2 * nz].sum(axis=0)
        send_totals(6)
        wait_all(top_recv.at[pl.ds(0, nz)], top_sem.at[0])
        top_total[0:2] = top_recv[0:nz].sum(axis=0)
        send_totals(7, 8)

        wait_totals(7)
        make_top(top_total[1], [top_total[2], top_total[3]], top_halo[...])

        @pl.when(rows_in)
        def _():
            wait_all(edge_recv.at[pl.ds(0, chips), pl.ds(0, 1)], edge_in.at[2])
            side_high[0:1] = edge_recv[:, 0:1].sum(axis=0)

        send_totals(4)
        sent = 2 * (chips - 1) + 2 * (nz - 1)
        pl.when(~rows_out)(lambda: wait_all(cells.at[pl.ds(0, sent // tiles)], out_sem))
        pl.when(rows_out)(lambda: wait_all(cells.at[pl.ds(0, (sent + chips // 8) // tiles)], out_sem))
        for send, (out, count) in enumerate(((~last, 3), (chip > 0, 3), (~top, 2))):
            pl.when(out)(lambda: wait_all(top_total.at[pl.ds(0, count)], edge_out.at[send]))
        wait_totals(1, 2, 9)
        make_side(True)
        pl.when(passes)(lambda: wait_all(side_high.at[pl.ds(0, 1)], edge_out.at[3]))
        wait_all(top_part.at[pl.ds(0, 3)], edge_out.at[4])
        pl.when(next_out)(lambda: wait_all(top_total.at[pl.ds(0, 2)], edge_out.at[5]))
        pl.when(first_out)(lambda: wait_all(side_next, edge_out.at[5]))


def unpack(maps, side_out, top_out):
    for i in range(3):
        side_out[i, :, 0:128] = maps[2 * i, :4]
        side_out[i, :, 128:256] = maps[2 * i + 1, :4]
        top_out[i, 0:8, :] = maps[6 + 2 * i, :, :64]
        top_out[i, 8:16, :] = maps[7 + 2 * i, :, :64]


def solution(mesh):
    ny, nz = mesh.shape["gy"], mesh.shape["gz"]
    chips = ny // 2

    def body(density):
        rows, depth, width = density.shape

        def blocks(*count):
            return pltpu.VMEM((*count, 8, 128), jnp.float32)

        vmem = pl.BlockSpec(memory_space=pltpu.VMEM)
        maps = pl.pallas_call(
            functools.partial(kernel, ny, nz, 1.0 / math.sqrt(depth * ny), 1.0 / math.sqrt(width * nz)),
            out_shape=pltpu.VMEM((12, 8, 128), jnp.float32),
            in_specs=[pl.BlockSpec(memory_space=pltpu.HBM)],
            out_specs=vmem,
            scratch_shapes=[
                pltpu.VMEM((rows, depth, width), jnp.float32),
                blocks(chips, 2),
                blocks(chips, 2),
                blocks(chips, 2),
                blocks(2),
                blocks(2),
                blocks(),
                blocks(),
                blocks(),
                blocks(chips),
                blocks(chips),
                blocks(CHUNKS),
                blocks(nz, 2),
                blocks(2 * nz, 2),
                blocks(4),
                blocks(),
                pltpu.SemaphoreType.DMA((len(LOADS),)),
                pltpu.SemaphoreType.DMA((3,)),
                pltpu.SemaphoreType.DMA,
                pltpu.SemaphoreType.DMA,
                pltpu.SemaphoreType.DMA((2,)),
                pltpu.SemaphoreType.DMA((6,)),
                pltpu.SemaphoreType.DMA((4,)),
                pltpu.SemaphoreType.REGULAR,
                pltpu.SemaphoreType.REGULAR,
            ],
            compiler_params=pltpu.CompilerParams(
                collective_id=0, has_side_effects=True, vmem_limit_bytes=16 * 1024 * 1024
            ),
            name="views",
        )(pltpu.with_memory_space_constraint(density, pltpu.HBM))
        side, top = pl.pallas_call(
            unpack,
            out_shape=(
                jax.ShapeDtypeStruct((3, rows // ny, width), jnp.float32),
                jax.ShapeDtypeStruct((3, depth, rows // nz), jnp.float32),
            ),
            in_specs=[vmem],
            out_specs=(vmem, vmem),
            name="unpack",
        )(pltpu.with_memory_space_constraint(maps, pltpu.VMEM))
        return side, jnp.swapaxes(top, 1, 2)

    return jax.shard_map(
        body,
        mesh=mesh,
        in_specs=(P(None, "gy", "gz"),),
        out_specs=(P(None, "gy", "gz"), P(None, "gz", "gy")),
        check_vma=False,
    )
```
